512 devices in a mesh: tm: 8 (over z), lon: 16 (over x_hi, y), lat: 4 (over x_lo, core).
Axes of the slice: x: 4 (x_hi: 2, x_lo: 2; x = x_hi * 2 + x_lo), y: 8, z: 8, core: 2. Of those that a mesh axis runs over, the one named last changes fastest.
Arguments:
- features: bfloat16 [16, 32, 1024, 128], P('tm', 'lat', 'lon'), may hold values from -6 to 6
- conv_first: bfloat16 [3, 3, 3, 128, 128], replicated, may hold values from -0.109375 to 0.109375
- conv_second: bfloat16 [3, 3, 3, 128, 128], replicated, may hold values from -0.109375 to 0.109375
Outputs:
- decoded: bfloat16 [16, 32, 1024, 128], P('tm', 'lat', 'lon')
The draws below stay inside these ranges and needn't reach their ends.
All inputs are finite; a program needn't handle non-finite values.
Results may differ from the reference program's by a relative error of at most 0.003.
Values may be sent and summed in bfloat16 or wider, within the bound.
A program may use at most 64 MiB of HBM per device.

```python
import jax
import jax.numpy as jnp
from jax import lax

C = 128
FRAMES = 16
NLAT = 32
NLON = 1024


def steps_of(own_key, extent, pieces, smallest, largest):
    loudness, own = 1.0, jax.random.fold_in(own_key, 6)
    for axis_at, parts in pieces:
        heights = jnp.exp(jax.random.uniform(jax.random.fold_in(own, axis_at), (parts,), jnp.float32, smallest / len(pieces), largest / len(pieces)))
        loudness = loudness * jnp.repeat(heights, extent[axis_at] // parts).reshape([-1 if axis == axis_at else 1 for axis in range(len(extent))])
    return loudness


def normal_values(key, extent, width, limit, shards=(), held_as=jnp.bfloat16):
    values = jax.random.normal(key, extent, jnp.float32) * width
    if len(shards) > 0:
        values = steps_of(key, extent, shards, -0.22, 0.18) * values
    return jnp.clip(values, min=-limit, max=limit).astype(held_as)


def setup_inputs(seed: int = 0) -> dict:
    arg_keys = jax.random.split(jax.random.key(seed), 4)
    features = normal_values(arg_keys[0], (FRAMES, NLAT, NLON, C), 1.0, 6.0, ((0, 8), (1, 4), (2, 16)))
    conv_first = normal_values(arg_keys[1], (3, 3, 3, C, C), (27 * C) ** -0.5, 0.109375)
    conv_second = normal_values(arg_keys[2], (3, 3, 3, C, C), (27 * C) ** -0.5, 0.109375)
    return dict(features=features, conv_first=conv_first, conv_second=conv_second)


def causal_conv(volume, kernel):
    padded = jnp.pad(volume, ((2, 0), (1, 1), (0, 0), (0, 0)))
    padded = jnp.concatenate([padded[:, :, -1:], padded, padded[:, :, :1]], axis=2)
    result = lax.conv_general_dilated(padded[None], kernel, (1, 1, 1), "VALID", dimension_numbers=("NDHWC", "DHWIO", "NDHWC"), preferred_element_type=jnp.float32)
    return result[0]


def reference(features, conv_first, conv_second):
    hidden = jax.nn.silu(causal_conv(features, conv_first)).astype(jnp.bfloat16)
    summed = features.astype(jnp.float32) + causal_conv(hidden, conv_second)
    return summed.astype(jnp.bfloat16)
```

```python
import jax
import jax.numpy as jnp
from jax import lax
from jax.experimental import pallas as pl
from jax.experimental.pallas import tpu as pltpu
from jax.sharding import PartitionSpec as P

MESH = pl.DeviceIdType.MESH
BF16, F32 = jnp.bfloat16, jnp.float32
F0P, F1P, F0, F1, H0P, H1P, H0, H1 = range(8)
NEXT = {F0: F0P, F1: F1P, H0: H0P, H1: H1P}


def block(groups, tiles_lon, tiles_lat, f_ref, k1_ref, k2_ref, o_ref, xc, xl, xr, pack, rim, w1, w2, acc, out,
          zsend, zrecv, lsend, lrecv, load, store):
    tm, lon, lat = lax.axis_index("tm"), lax.axis_index("lon"), lax.axis_index("lat")
    rows, cols, chan = f_ref.shape[1:]
    spots = rows * cols
    east, west = lax.rem(lon + 1, tiles_lon), lax.rem(lon + tiles_lon - 1, tiles_lon)
    has_prev, has_next, has_up, has_down = tm > 0, tm < groups - 1, lat > 0, lat < tiles_lat - 1

    barrier = pltpu.get_barrier_semaphore()

    def greet(**device):
        pl.semaphore_signal(barrier, inc=1, device_id=device, device_id_type=MESH)

    greet(lon=east)
    greet(lon=west)

    @pl.when(has_prev)
    def _():
        greet(tm=tm - 1)

    @pl.when(has_up)
    def _():
        for to in (lon, east, west):
            greet(lat=lat - 1, lon=to)

    @pl.when(has_down)
    def _():
        for to in (lon, east, west):
            greet(lat=lat + 1, lon=to)

    loads = [
        pltpu.make_async_copy(f_ref.at[1], xc.at[F1, pl.ds(1, rows)], load.at[0]),
        pltpu.make_async_copy(f_ref.at[0], xc.at[F0, pl.ds(1, rows)], load.at[1]),
        pltpu.make_async_copy(k1_ref, w1, load.at[2]),
        pltpu.make_async_copy(k2_ref, w2, load.at[3]),
    ]
    for copy in loads:
        copy.start()

    @pl.when(jnp.logical_not(has_prev))
    def _():
        for s in (F0P, F1P, H0P, H1P):
            xc[s] = jnp.zeros(xc.shape[1:], BF16)
            rim[s] = jnp.zeros(rim.shape[1:], BF16)

    @pl.when(jnp.logical_not(has_up))
    def _():
        for s in range(8):
            xc[s, 0] = jnp.zeros((cols, chan), BF16)
            rim[s, 2:4] = jnp.zeros((2, 16, chan), BF16)

    @pl.when(jnp.logical_not(has_down))
    def _():
        for s in range(8):
            xc[s, rows + 1] = jnp.zeros((cols, chan), BF16)
            rim[s, 4:6] = jnp.zeros((2, 16, chan), BF16)

    def remote(src, dst, sems, i, **device):
        return lambda: pltpu.make_async_remote_copy(
            src_ref=src, dst_ref=dst, send_sem=sems[0].at[i], recv_sem=sems[1].at[i],
            device_id=device, device_id_type=MESH)

    def forward(s):
        d, z = NEXT[s], (zsend, zrecv)
        i = 4 * (d if d < F0 else d - 2)
        to = lax.rem(tm + 1, groups)
        inner = pl.ds(2, rows - 2)
        return [
            remote(pack.at[s], pack.at[d], z, i, tm=to),
            remote(xc.at[s, 1], xc.at[d, 1], z, i + 1, tm=to),
            remote(xc.at[s, rows], xc.at[d, rows], z, i + 2, tm=to),
            remote(xc.at[s, inner], xc.at[d, inner], z, i + 3, tm=to),
        ]

    def sideways(s):
        z, i = (lsend, lrecv), 8 * s
        up, down = lax.rem(lat + tiles_lat - 1, tiles_lat), lax.rem(lat + 1, tiles_lat)
        return (
            [
                remote(pack.at[s], rim.at[s, 0], z, i, lon=east),
                remote(pack.at[s], rim.at[s, 1], z, i + 1, lon=west),
            ],
            [
                remote(xc.at[s, 1], xc.at[s, rows + 1], z, i + 2, lat=up),
                remote(pack.at[s], rim.at[s, 4], z, i + 3, lat=up, lon=east),
                remote(pack.at[s], rim.at[s, 5], z, i + 4, lat=up, lon=west),
            ],
            [
                remote(xc.at[s, rows], xc.at[s, 0], z, i + 5, lat=down),
                remote(pack.at[s], rim.at[s, 2], z, i + 6, lat=down, lon=east),
                remote(pack.at[s], rim.at[s, 3], z, i + 7, lat=down, lon=west),
            ],
        )

    def when_past(s, run):
        if s in (F0P, F1P, H0P, H1P):
            pl.when(has_prev)(run)
        else:
            run()

    def each(copies, method):
        for copy in copies:
            getattr(copy(), method)()

    def spread(s, method):
        def run():
            along, above, below = sideways(s)
            sent = method != "wait_recv"
            each(along, method)
            pl.when(has_up if sent else has_down)(lambda: each(above, method))
            pl.when(has_down if sent else has_up)(lambda: each(below, method))
        when_past(s, run)

    def send_on(s, method):
        pl.when(has_next)(lambda: each(forward(s), method))

    def edges_in(s):
        def run():
            each(forward(s)[:3], "wait_recv")
        pl.when(has_prev)(run)
        spread(NEXT[s], "start")

    def inner_in(s):
        pl.when(has_prev)(lambda: each(forward(s)[3:], "wait_recv"))

    def pack_of(x):
        return jnp.concatenate([x[r, j:j + 1] for j in (0, cols - 1) for r in range(rows)], axis=0)

    def shift(s):
        spread(s, "wait_recv")
        for r in range(rows + 2):
            if r == 0:
                left, right = rim[s, 2, 2 * rows - 1:], rim[s, 3, rows - 1:rows]
            elif r == rows + 1:
                left, right = rim[s, 4, rows:rows + 1], rim[s, 5, 0:1]
            else:
                left, right = rim[s, 0, rows + r - 1:rows + r], rim[s, 1, r - 1:r]
            x = xc[s, r]
            xl[s, r] = jnp.concatenate([left, x[:cols - 1]], axis=0)
            xr[s, r] = jnp.concatenate([x[1:], right], axis=0)

    def taps(s, w, times):
        left = jnp.concatenate(
            [ref[s, b:b + rows].reshape(spots, chan) for b in range(3) for ref in (xl, xc, xr)], axis=1)
        right = jnp.concatenate([w[a].reshape(9 * chan, chan) for a in times], axis=1)
        return jnp.dot(left, right, preferred_element_type=F32)

    def silu(v):
        return (v / (1 + jnp.exp(-v))).astype(BF16)

    def make_hidden(s, v):
        h = silu(v).reshape(rows, cols, chan)
        xc[s, 1:rows + 1] = h
        pack[s] = pack_of(h)
        send_on(s, "start")
        spread(s, "start")

    for s, copy in ((F1, loads[0]), (F0, loads[1])):
        copy.wait()
        pack[s] = pack_of(xc[s, 1:rows + 1])
    pl.semaphore_wait(
        barrier, 2 + has_next.astype(jnp.int32) + 3 * has_up.astype(jnp.int32) + 3 * has_down.astype(jnp.int32))

    for s in (F1, F0):
        send_on(s, "start")
    for s in (F1, F0):
        spread(s, "start")
    loads[2].wait()
    edges_in(F1)
    shift(F1)
    acc[:, chan:] = taps(F1, w1, (2,))
    shift(F0)
    v = taps(F0, w1, (2, 1))
    acc[:, :chan] = v[:, :chan]
    acc[:, chan:] += v[:, chan:]
    edges_in(F0)
    inner_in(F1)
    shift(F1P)
    v = acc[...] + taps(F1P, w1, (1, 0))
    acc[:, :chan] = v[:, :chan]
    make_hidden(H1, v[:, chan:])
    inner_in(F0)
    shift(F0P)
    make_hidden(H0, acc[:, :chan] + taps(F0P, w1, (0,)))

    loads[3].wait()
    edges_in(H1)
    shift(H1)
    acc[:, chan:] = xc[F1, 1:rows + 1].reshape(spots, chan).astype(F32) + taps(H1, w2, (2,))
    edges_in(H0)
    shift(H0)
    v = taps(H0, w2, (2, 1))
    acc[:, :chan] = xc[F0, 1:rows + 1].reshape(spots, chan).astype(F32) + v[:, :chan]
    acc[:, chan:] += v[:, chan:]
    for s in (F1, F0, H1, H0):
        send_on(s, "wait_send")
    for s in (F1, F0, F1P, F0P, H1, H0, H1P):
        spread(s, "wait_send")
    inner_in(H1)
    shift(H1P)
    v = acc[...] + taps(H1P, w2, (1, 0))
    acc[:, :chan] = v[:, :chan]
    out[1] = v[:, chan:].astype(BF16).reshape(rows, cols, chan)
    stores = [pltpu.make_async_copy(out.at[t], o_ref.at[t], store.at[t]) for t in range(2)]
    stores[1].start()
    inner_in(H0)
    shift(H0P)
    out[0] = (acc[:, :chan] + taps(H0P, w2, (0,))).astype(BF16).reshape(rows, cols, chan)
    stores[0].start()
    spread(H0P, "wait_send")
    for copy in stores:
        copy.wait()


def solution(mesh):
    groups, tiles_lon, tiles_lat = mesh.shape["tm"], mesh.shape["lon"], mesh.shape["lat"]

    def local(features, conv_first, conv_second):
        frames, rows, cols, chan = features.shape
        frame = (8, rows + 2, cols, chan)

        def kernel(*refs):
            block(groups, tiles_lon, tiles_lat, *refs)

        return pl.pallas_call(
            kernel,
            out_shape=jax.ShapeDtypeStruct(features.shape, BF16),
            in_specs=[pl.BlockSpec(memory_space=pl.ANY)] * 3,
            out_specs=pl.BlockSpec(memory_space=pl.ANY),
            scratch_shapes=[
                pltpu.VMEM(frame, BF16),
                pltpu.VMEM(frame, BF16),
                pltpu.VMEM(frame, BF16),
                pltpu.VMEM((8, 2 * rows, chan), BF16),
                pltpu.VMEM((8, 6, 2 * rows, chan), BF16),
                pltpu.VMEM(conv_first.shape, BF16),
                pltpu.VMEM(conv_second.shape, BF16),
                pltpu.VMEM((rows * cols, 2 * chan), F32),
                pltpu.VMEM(features.shape, BF16),
                pltpu.SemaphoreType.DMA((16,)),
                pltpu.SemaphoreType.DMA((16,)),
                pltpu.SemaphoreType.DMA((64,)),
                pltpu.SemaphoreType.DMA((64,)),
                pltpu.SemaphoreType.DMA((4,)),
                pltpu.SemaphoreType.DMA((2,)),
            ],
            compiler_params=pltpu.CompilerParams(
                collective_id=0, has_side_effects=True, vmem_limit_bytes=32 * 2**20),
            cost_estimate=pl.CostEstimate(flops=2 * 2 * 1024 * 27 * chan * chan, bytes_accessed=3 * 2**20, transcendentals=2**17),
            name="conv_block",
        )(features, conv_first, conv_second)

    placed = P("tm", "lat", "lon", None)
    return jax.shard_map(local, mesh=mesh, in_specs=(placed, P(), P()), out_specs=placed, check_vma=False)
```

```python
import jax
import jax.numpy as jnp
from jax import lax
from jax.experimental import pallas as pl
from jax.experimental.pallas import tpu as pltpu
from jax.sharding import PartitionSpec as P

MESH = pl.DeviceIdType.MESH
BF16, F32, I32 = jnp.bfloat16, jnp.float32, jnp.int32
F0P, F1P, F0, F1, H0P, H1P, H0, H1 = range(8)
NEXT = {F0: F0P, F1: F1P, H0: H0P, H1: H1P}
E, W, U, UE, UW, D, DE, DW = range(8)
STEP = {E: (1, 0), W: (-1, 0), U: (0, -1), UE: (1, -1), UW: (-1, -1), D: (0, 1), DE: (1, 1), DW: (-1, 1)}
BACK = {E: W, W: E, U: D, D: U, UE: DW, DW: UE, UW: DE, DE: UW}
RIM = {E: 0, W: 1, DE: 2, DW: 3, UE: 4, UW: 5}
T = 16


def block(groups, tiles_lon, tiles_lat, f_ref, k1_ref, k2_ref, o_ref, xc, xl, xr, pack, rim, halo, w1, w2,
          acc_in, acc_out, acc, zsend, zrecv, lsend, lrecv, load, entered):
    tm, lon, lat = lax.axis_index("tm"), lax.axis_index("lon"), lax.axis_index("lat")
    rows, cols, chan = f_ref.shape[1:]
    has_prev, has_next, has_up, has_down = tm > 0, tm < groups - 1, lat > 0, lat < tiles_lat - 1

    ring = tiles_lon // 2

    def lateness(at):
        y = lax.rem(at, ring)
        return jnp.minimum(y, ring - y)

    east, west = lax.rem(lon + 1, tiles_lon), lax.rem(lon + tiles_lon - 1, tiles_lon)
    earlier_e, earlier_w = lateness(east) < lateness(lon), lateness(west) < lateness(lon)
    later_e, later_w = jnp.logical_not(earlier_e), jnp.logical_not(earlier_w)
    far_e, far_w = lax.rem(lon, ring) == ring - 1, lax.rem(lon, ring) == 0
    near_e, near_w = jnp.logical_not(far_e), jnp.logical_not(far_w)
    far = jnp.logical_or(far_e, far_w)
    up, down = lax.rem(lat + tiles_lat - 1, tiles_lat), lax.rem(lat + 1, tiles_lat)

    def device(d):
        step_lon, step_lat = STEP[d]
        to = {}
        if step_lon:
            to["lon"] = east if step_lon > 0 else west
        if step_lat:
            to["lat"] = down if step_lat > 0 else up
        return to

    def toward(ds, *runs):
        def some(rise):
            return [d for d in ds if STEP[d][1] == rise]

        def all_of(ds):
            for run in runs:
                for d in ds:
                    run(d)

        all_of(some(0))
        for rise, cond in ((-1, has_up), (1, has_down)):
            if some(rise):
                pl.when(cond)(lambda rise=rise: all_of(some(rise)))

    barrier = pltpu.get_barrier_semaphore()

    def greet(d):
        pl.semaphore_signal(barrier, inc=1, device_id=device(d), device_id_type=MESH)

    @pl.when(has_prev)
    def _():
        pl.semaphore_signal(barrier, inc=1, device_id={"tm": tm - 1}, device_id_type=MESH)

    toward((U, D, W), greet)
    pl.when(near_e)(lambda: greet(E))
    pl.when(later_e)(lambda: toward((UE, DE), greet))
    pl.when(later_w)(lambda: toward((UW, DW), greet))

    loads = [
        pltpu.make_async_copy(f_ref.at[1], xc.at[F1, pl.ds(1, rows)], load.at[0]),
        pltpu.make_async_copy(f_ref.at[0], xc.at[F0, pl.ds(1, rows)], load.at[1]),
        pltpu.make_async_copy(k1_ref, w1, load.at[2]),
        pltpu.make_async_copy(k2_ref, w2, load.at[3]),
    ]
    for copy in loads:
        copy.start()

    def remote(src, dst, sems, i, to):
        return pltpu.make_async_remote_copy(
            src_ref=src, dst_ref=dst, send_sem=sems[0].at[i], recv_sem=sems[1].at[i], device_id=to, device_id_type=MESH)

    body, both, past = pl.ds(1, rows), pl.ds(F0, 2), pl.ds(F0P, 2)
    left, inner, right = pl.ds(0, T), pl.ds(T, cols - 2 * T), pl.ds(cols - T, T)

    PACKS, F1_TOP, F1_LOW, F1_MID, F0_TOP, F0_LOW, F0_MID = range(7)
    H1_HALO, H1_IN, H1_LEFT, H1_RIGHT, H0_HALO, H0_TOP, H0_LOW, H0_MID = range(7, 15)

    def forward(i):
        def at(s, *where):
            return xc.at[(s, *where)], xc.at[(NEXT[s], *where)]

        mid = pl.ds(2, rows - 2)
        src, dst = {
            PACKS: lambda: (pack.at[both], pack.at[past]),
            F1_TOP: lambda: at(F1, 1), F1_LOW: lambda: at(F1, rows), F1_MID: lambda: at(F1, mid),
            F0_TOP: lambda: at(F0, 1), F0_LOW: lambda: at(F0, rows), F0_MID: lambda: at(F0, mid),
            H1_HALO: lambda: (halo.at[H1 - 4, 0], halo.at[H1P - 4, 0]),
            H1_IN: lambda: at(H1, body, inner), H1_LEFT: lambda: at(H1, body, left), H1_RIGHT: lambda: at(H1, body, right),
            H0_HALO: lambda: (halo.at[H0 - 4, 0], halo.at[H0P - 4, 0]),
            H0_TOP: lambda: at(H0, 1), H0_LOW: lambda: at(H0, rows), H0_MID: lambda: at(H0, mid),
        }[i]()
        return remote(src, dst, (zsend, zrecv), i, {"tm": lax.rem(tm + 1, groups)})

    def send_on(*parts):
        pl.when(has_next)(lambda: [forward(p).start() for p in parts] and None)

    def arrived(*parts):
        pl.when(has_prev)(lambda: [forward(p).wait_recv() for p in parts] and None)

    def own(d):
        if d in RIM:
            src, dst = pack.at[both, int(STEP[d][0] > 0)], rim.at[both, RIM[d]]
        else:
            src, dst = xc.at[both, 1 if d == U else rows], xc.at[both, rows + 1 if d == U else 0]
        return remote(src, dst, (lsend, lrecv), d, device(d))

    def past_pack(d):
        return remote(pack.at[past, int(STEP[d][0] > 0)], rim.at[past, RIM[d]], (lsend, lrecv), 8 + d, device(d))

    def row(s):
        base = {F1P: 8, F0P: 16}.get(s, 24 + 4 * (s - 4))

        def make(d):
            return remote(
                xc.at[s, 1 if d == U else rows], xc.at[s, rows + 1 if d == U else 0],
                (lsend, lrecv), base + (d if s < H0P else int(d == D)), device(d))
        return make

    def halo_of(s):
        def make(d):
            return remote(
                halo.at[s - 4, 0], halo.at[s - 4, 2 if d == U else 1],
                (lsend, lrecv), 26 + 4 * (s - 4) + int(d == D), device(d))
        return make

    def send(*makes):
        return [lambda d, make=make: make(d).start() for make in makes]

    def receive(*makes):
        return [lambda d, make=make: make(BACK[d]).wait_recv() for make in makes]

    def sent(*makes):
        return [lambda d, make=make: make(d).wait_send() for make in makes]

    def if_past(run):
        pl.when(has_prev)(run)

    ROWS, SIDES = (U, D), (E, UE, DE, W, UW, DW)

    @pl.when(jnp.logical_not(has_prev))
    def _():
        for s in (F0P, F1P, H0P, H1P):
            xc[s] = jnp.zeros(xc.shape[1:], BF16)
        pack[past] = jnp.zeros((2, *pack.shape[1:]), BF16)
        rim[past] = jnp.zeros((2, *rim.shape[1:]), BF16)
        halo[0:2] = jnp.zeros((2, *halo.shape[1:]), BF16)

    @pl.when(jnp.logical_not(has_up))
    def _():
        for s in range(8):
            xc[s, 0] = jnp.zeros((cols, chan), BF16)
        for s in range(4):
            rim[s, 2:4] = jnp.zeros((2, 2 * rows, chan), BF16)
            halo[s, 1] = jnp.zeros((2 * rows, chan), BF16)

    @pl.when(jnp.logical_not(has_down))
    def _():
        for s in range(8):
            xc[s, rows + 1] = jnp.zeros((cols, chan), BF16)
        for s in range(4):
            rim[s, 4:6] = jnp.zeros((2, 2 * rows, chan), BF16)
            halo[s, 2] = jnp.zeros((2 * rows, chan), BF16)

    def make_pack(s):
        for half, at in ((0, 0), (1, cols - T)):
            tile = [xc[s, r, at:at + T] for r in range(1, rows + 1)]
            js = (0, 1) if half == 0 else (T - 2, T - 1)
            pack[s, half] = jnp.concatenate([x[j:j + 1] for j in js for x in tile], axis=0)

    def beside(s, r):
        if s < H0P:
            if r == 0:
                return rim[s, 2, 2 * rows - 1:], rim[s, 3, rows - 1:rows]
            if r == rows + 1:
                return rim[s, 4, rows:rows + 1], rim[s, 5, 0:1]
            return rim[s, 0, rows + r - 1:rows + r], rim[s, 1, r - 1:r]
        if r == 0:
            return halo[s - 4, 1, rows - 1:rows], halo[s - 4, 1, 2 * rows - 1:]
        if r == rows + 1:
            return halo[s - 4, 2, 0:1], halo[s - 4, 2, rows:rows + 1]
        return halo[s - 4, 0, r - 1:r], halo[s - 4, 0, rows + r - 1:rows + r]

    def shift_in(s):
        for r in range(rows + 2):
            x = xc[s, r]
            xl[s, r, T:cols - T] = x[T - 1:cols - T - 1]
            xr[s, r, T:cols - T] = x[T + 1:cols - T + 1]

    def shift_out(s):
        for r in range(rows + 2):
            before, after = beside(s, r)
            x = xc[s, r]
            xl[s, r, 0:T] = jnp.concatenate([before, x[:T - 1]], axis=0)
            xl[s, r, cols - T:] = x[cols - T - 1:cols - 1]
            xr[s, r, 0:T] = x[1:T + 1]
            xr[s, r, cols - T:] = jnp.concatenate([x[cols - T + 1:], after], axis=0)

    def shift_all(s):
        for r in range(rows + 2):
            before, after = beside(s, r)
            x = xc[s, r]
            xl[s, r] = jnp.concatenate([before, x[:cols - 1]], axis=0)
            xr[s, r] = jnp.concatenate([x[1:], after], axis=0)

    def halo_taps(s):
        def column(above, mid, below):
            above, mid, below = above.astype(F32), mid.astype(F32), below.astype(F32)
            return (jnp.concatenate([above, mid[:rows - 1]], axis=0), mid, jnp.concatenate([mid[1:], below], axis=0))

        def rim_column(at, side):
            k = side
            return column(rim[s, k + 2, at + rows - 1:at + rows], rim[s, k, at:at + rows], rim[s, k + 4, at:at + 1])

        first = column(xc[s, 0, 0:1], pack[s, 0, 0:rows], xc[s, rows + 1, 0:1])
        last = column(xc[s, 0, cols - 1:], pack[s, 1, rows:], xc[s, rows + 1, cols - 1:])
        wests = (rim_column(0, 0), rim_column(rows, 0), first)
        easts = (last, rim_column(0, 1), rim_column(rows, 1))
        return jnp.concatenate(
            [jnp.concatenate([wests[c][b], easts[c][b]], axis=0).astype(BF16) for b in range(3) for c in range(3)], axis=1)

    IN, OUT, ALL = (slice(T, cols - T),), (slice(0, T), slice(cols - T, cols)), (slice(0, cols),)

    def taken(ref, s, b, cuts):
        some = [ref[s, b:b + rows, c] for c in cuts]
        some = some[0] if len(some) == 1 else jnp.concatenate(some, axis=1)
        return some.reshape(-1, chan)

    def taps(s, w, times, cuts):
        x = jnp.concatenate([taken(ref, s, b, cuts) for b in range(3) for ref in (xl, xc, xr)], axis=1)
        if cuts is OUT:
            x = jnp.concatenate([x, halo_taps(s)], axis=0)
        k = jnp.concatenate([w[a].reshape(9 * chan, chan) for a in times], axis=1)
        return jnp.dot(x, k, preferred_element_type=F32)

    def shift(s, cuts):
        (shift_in if cuts is IN else shift_out if cuts is OUT else shift_all)(s)

    def own_frames(later, earlier, w, acc, cuts):
        shift(later, cuts)
        shift(earlier, cuts)
        v = taps(earlier, w, (2, 1), cuts)
        acc[:, :chan] = v[:, :chan]
        acc[:, chan:] = v[:, chan:] + taps(later, w, (2,), cuts)

    def past_later(s, w, acc, cuts):
        shift(s, cuts)
        v = acc[...] + taps(s, w, (1, 0), cuts)
        acc[:, :chan] = v[:, :chan]
        return v[:, chan:]

    def past_earlier(s, w, acc, cuts):
        shift(s, cuts)
        return acc[:, :chan] + taps(s, w, (0,), cuts)

    def silu(v):
        return (v / (1 + jnp.exp(-v))).astype(BF16)

    def hidden_in(s, v):
        xc[s, 1:rows + 1, T:cols - T] = silu(v).reshape(rows, cols - 2 * T, chan)

    def hidden_out(s, v):
        h = silu(v)
        halo[s - 4, 0] = h[2 * T * rows:]
        h = h[:2 * T * rows].reshape(rows, 2 * T, chan)
        xc[s, 1:rows + 1, 0:T] = h[:, :T]
        xc[s, 1:rows + 1, cols - T:] = h[:, T:]

    def result(t, v):
        x = xc[(F0, F1)[t], 1:rows + 1].reshape(-1, chan).astype(F32) + v
        o_ref[t] = x.astype(BF16).reshape(rows, cols, chan)

    for s, copy in ((F1, loads[0]), (F0, loads[1])):
        copy.wait()
        make_pack(s)

    heights = has_up.astype(I32) + has_down.astype(I32)
    pl.semaphore_wait(
        barrier,
        1 + has_next.astype(I32) + near_w.astype(I32) + heights * (1 + earlier_e.astype(I32) + earlier_w.astype(I32)))

    send_on(PACKS, F1_TOP, F1_LOW, F1_MID, F0_TOP, F0_LOW, F0_MID)

    def tell(d):
        pl.semaphore_signal(entered.at[BACK[d]], inc=1, device_id=device(d), device_id_type=MESH)

    def told(d):
        pl.semaphore_wait(entered.at[d], 1)

    pl.when(far_e)(lambda: tell(E))
    pl.when(earlier_e)(lambda: toward((UE, DE), tell))
    pl.when(earlier_w)(lambda: toward((UW, DW), tell))

    def known(*runs, rows=()):
        toward((E, *rows), *runs)
        pl.when(near_w)(lambda: toward((W,), *runs))
        pl.when(earlier_e)(lambda: toward((UE, DE), *runs))
        pl.when(earlier_w)(lambda: toward((UW, DW), *runs))

    def send_past_pack(d):
        if_past(lambda: past_pack(d).start())

    def after_word(ds):
        toward(ds, told, *send(own), send_past_pack)

    known(*send(own), rows=ROWS)
    arrived(PACKS)
    if_past(lambda: known(*send(past_pack)))
    arrived(F1_TOP, F1_LOW)
    if_past(lambda: toward(ROWS, *send(row(F1P))))
    loads[2].wait()
    toward(ROWS, *receive(own))
    own_frames(F1, F0, w1, acc_in, IN)
    pl.when(later_e)(lambda: after_word((UE, DE)))
    pl.when(jnp.logical_and(later_w, near_w))(lambda: after_word((UW, DW)))
    arrived(F1_MID)
    if_past(lambda: toward(ROWS, *receive(row(F1P))))
    hidden_in(H1, past_later(F1P, w1, acc_in, IN))
    send_on(H1_IN)
    arrived(F0_TOP, F0_LOW)
    if_past(lambda: toward(ROWS, *send(row(F0P))))
    pl.when(far_w)(lambda: after_word((W, UW, DW)))

    def outer_later():
        toward(SIDES, *receive(own))
        own_frames(F1, F0, w1, acc_out, OUT)
        if_past(lambda: toward(SIDES, *receive(past_pack)))
        hidden_out(H1, past_later(F1P, w1, acc_out, OUT))
        send_on(H1_HALO, H1_LEFT, H1_RIGHT)
        toward(ROWS, *send(row(H1), halo_of(H1)))

    pl.when(jnp.logical_not(far))(outer_later)
    arrived(F0_MID)
    if_past(lambda: toward(ROWS, *receive(row(F0P))))
    hidden_in(H0, past_earlier(F0P, w1, acc_in, IN))
    pl.when(far)(outer_later)
    hidden_out(H0, past_earlier(F0P, w1, acc_out, OUT))
    send_on(H0_HALO, H0_TOP, H0_LOW, H0_MID)
    toward(ROWS, *send(row(H0), halo_of(H0)))

    loads[3].wait()
    arrived(H1_HALO, H1_IN, H1_LEFT, H1_RIGHT)
    if_past(lambda: toward(ROWS, *send(row(H1P), halo_of(H1P))))
    toward(ROWS, *receive(row(H1), row(H0), halo_of(H1), halo_of(H0)))
    own_frames(H1, H0, w2, acc, ALL)
    arrived(H0_HALO, H0_TOP, H0_LOW)
    if_past(lambda: toward(ROWS, *send(row(H0P), halo_of(H0P))))
    if_past(lambda: toward(ROWS, *receive(row(H1P), halo_of(H1P))))
    result(1, past_later(H1P, w2, acc, ALL))
    pl.when(has_next)(lambda: [forward(p).wait_send() for p in range(15)] and None)
    toward(ROWS + SIDES, *sent(own))
    toward(ROWS, *sent(row(H0), halo_of(H0), row(H1), halo_of(H1)))

    @pl.when(has_prev)
    def _():
        toward(SIDES, *sent(past_pack))
        toward(ROWS, *sent(row(F1P), row(F0P), row(H1P), halo_of(H1P)))

    arrived(H0_MID)
    if_past(lambda: toward(ROWS, *receive(row(H0P), halo_of(H0P))))
    result(0, past_earlier(H0P, w2, acc, ALL))
    if_past(lambda: toward(ROWS, *sent(row(H0P), halo_of(H0P))))


def solution(mesh):
    groups, tiles_lon, tiles_lat = mesh.shape["tm"], mesh.shape["lon"], mesh.shape["lat"]

    def local(features, conv_first, conv_second):
        frames, rows, cols, chan = features.shape
        frame = (8, rows + 2, cols, chan)
        outer = 2 * T * rows + 2 * rows

        def kernel(*refs):
            block(groups, tiles_lon, tiles_lat, *refs)

        return pl.pallas_call(
            kernel,
            out_shape=pltpu.VMEM(features.shape, BF16),
            in_specs=[pl.BlockSpec(memory_space=pltpu.HBM)] * 3,
            out_specs=pl.BlockSpec(memory_space=pltpu.VMEM),
            scratch_shapes=[
                pltpu.VMEM(frame, BF16),
                pltpu.VMEM(frame, BF16),
                pltpu.VMEM(frame, BF16),
                pltpu.VMEM((4, 2, 2 * rows, chan), BF16),
                pltpu.VMEM((4, 6, 2 * rows, chan), BF16),
                pltpu.VMEM((4, 3, 2 * rows, chan), BF16),
                pltpu.VMEM(conv_first.shape, BF16),
                pltpu.VMEM(conv_second.shape, BF16),
                pltpu.VMEM(((cols - 2 * T) * rows, 2 * chan), F32),
                pltpu.VMEM((outer, 2 * chan), F32),
                pltpu.VMEM((rows * cols, 2 * chan), F32),
                pltpu.SemaphoreType.DMA((15,)),
                pltpu.SemaphoreType.DMA((15,)),
                pltpu.SemaphoreType.DMA((40,)),
                pltpu.SemaphoreType.DMA((40,)),
                pltpu.SemaphoreType.DMA((4,)),
                pltpu.SemaphoreType.REGULAR((8,)),
            ],
            compiler_params=pltpu.CompilerParams(
                collective_id=0, has_side_effects=True, vmem_limit_bytes=32 * 2**20),
            cost_estimate=pl.CostEstimate(
                flops=4 * frames * rows * cols * 27 * chan * chan, bytes_accessed=3 * 2**20, transcendentals=2**17),
            name="conv_block",
        )(*(pltpu.with_memory_space_constraint(x, pltpu.HBM) for x in (features, conv_first, conv_second)))

    placed = P("tm", "lat", "lon", None)
    return jax.shard_map(local, mesh=mesh, in_specs=(placed, P(), P()), out_specs=placed, check_vma=False)
```

```python
import jax
import jax.numpy as jnp
from jax import lax
from jax.experimental import pallas as pl
from jax.experimental.pallas import tpu as pltpu
from jax.sharding import PartitionSpec as P

MESH = pl.DeviceIdType.MESH
BF16, F32, I32 = jnp.bfloat16, jnp.float32, jnp.int32
F0P, F1P, F0, F1, H0P, H1P, H0, H1 = range(8)
NEXT = {F0: F0P, F1: F1P, H0: H0P, H1: H1P}
E, W, U, UE, UW, D, DE, DW = range(8)
STEP = {E: (1, 0), W: (-1, 0), U: (0, -1), UE: (1, -1), UW: (-1, -1), D: (0, 1), DE: (1, 1), DW: (-1, 1)}
BACK = {E: W, W: E, U: D, D: U, UE: DW, DW: UE, UW: DE, DE: UW}
RIM = {E: 0, W: 1, DE: 2, DW: 3, UE: 4, UW: 5}
T = 16


def block(groups, tiles_lon, tiles_lat, f_ref, k1_ref, k2_ref, o_ref, xc, xl, xr, pack, rim, halo, w1, w2,
          acc_in, acc_out, acc, zsend, zrecv, lsend, lrecv, load, entered):
    tm, lon, lat = lax.axis_index("tm"), lax.axis_index("lon"), lax.axis_index("lat")
    rows, cols, chan = f_ref.shape[1:]
    has_prev, has_next, has_up, has_down = tm > 0, tm < groups - 1, lat > 0, lat < tiles_lat - 1

    ring = tiles_lon // 2

    def lateness(at):
        y = lax.rem(at, ring)
        return jnp.minimum(y, ring - y)

    east, west = lax.rem(lon + 1, tiles_lon), lax.rem(lon + tiles_lon - 1, tiles_lon)
    earlier_e, earlier_w = lateness(east) < lateness(lon), lateness(west) < lateness(lon)
    later_e, later_w = jnp.logical_not(earlier_e), jnp.logical_not(earlier_w)
    far_e, far_w = lax.rem(lon, ring) == ring - 1, lax.rem(lon, ring) == 0
    near_e, near_w = jnp.logical_not(far_e), jnp.logical_not(far_w)
    up, down = lax.rem(lat + tiles_lat - 1, tiles_lat), lax.rem(lat + 1, tiles_lat)

    def device(d):
        step_lon, step_lat = STEP[d]
        to = {}
        if step_lon:
            to["lon"] = east if step_lon > 0 else west
        if step_lat:
            to["lat"] = down if step_lat > 0 else up
        return to

    def toward(ds, *runs):
        def some(rise):
            return [d for d in ds if STEP[d][1] == rise]

        def all_of(ds):
            for run in runs:
                for d in ds:
                    run(d)

        all_of(some(0))
        for rise, cond in ((-1, has_up), (1, has_down)):
            if some(rise):
                pl.when(cond)(lambda rise=rise: all_of(some(rise)))

    barrier = pltpu.get_barrier_semaphore()

    def greet(d):
        pl.semaphore_signal(barrier, inc=1, device_id=device(d), device_id_type=MESH)

    @pl.when(has_prev)
    def _():
        pl.semaphore_signal(barrier, inc=1, device_id={"tm": tm - 1}, device_id_type=MESH)

    origin = jnp.logical_and(tm == 0, jnp.logical_and(lon == 0, lat == 0))
    awake = jnp.logical_not(origin)
    lon_of, lat_of = {0: lon, 1: east, -1: west}, {0: lat, 1: down, -1: up}

    def to_origin(d):
        x, y = STEP[d]
        return jnp.logical_and(tm == 0, jnp.logical_and(lon_of[x] == 0, lat_of[y] == 0))

    def either(a, b):
        return True if a is True or b is True else jnp.logical_or(a, b)

    def greets_me(d):
        first = {U: True, D: True, E: either(near_e, earlier_e), W: near_w}.get(d, earlier_e if STEP[d][0] > 0 else earlier_w)
        if d in (D, DE, DW):
            return either(origin, first)
        return jnp.logical_and(either(origin, first), jnp.logical_not(to_origin(d)))

    def i_greet(d):
        first = {U: True, D: True, E: near_e, W: True}.get(d, later_e if STEP[d][0] > 0 else later_w)
        if d in (D, DE, DW):
            return jnp.logical_and(awake, first)
        return jnp.logical_and(awake, either(first, to_origin(d)))

    def toward_if(cond, ds, *runs):
        toward(ds, *[lambda d, run=run: pl.when(cond(d))(lambda: run(d)) for run in runs])

    toward_if(i_greet, range(8), greet)

    loads = [
        pltpu.make_async_copy(f_ref.at[1], xc.at[F1, pl.ds(1, rows)], load.at[0]),
        pltpu.make_async_copy(f_ref.at[0], xc.at[F0, pl.ds(1, rows)], load.at[1]),
        pltpu.make_async_copy(k1_ref, w1, load.at[2]),
        pltpu.make_async_copy(k2_ref, w2, load.at[3]),
    ]
    for copy in loads:
        copy.start()

    def remote(src, dst, sems, i, to):
        return pltpu.make_async_remote_copy(
            src_ref=src, dst_ref=dst, send_sem=sems[0].at[i], recv_sem=sems[1].at[i], device_id=to, device_id_type=MESH)

    body, both, past = pl.ds(1, rows), pl.ds(F0, 2), pl.ds(F0P, 2)
    left, inner, right = pl.ds(0, T), pl.ds(T, cols - 2 * T), pl.ds(cols - T, T)

    PACKS, F1_TOP, F1_LOW, F1_MID, F0_TOP, F0_LOW, F0_MID = range(7)
    H1_HALO, H1_IN, H1_LEFT, H1_RIGHT, H0_HALO, H0_TOP, H0_LOW, H0_MID = range(7, 15)

    def forward(i):
        def at(s, *where):
            return xc.at[(s, *where)], xc.at[(NEXT[s], *where)]

        mid = pl.ds(2, rows - 2)
        src, dst = {
            PACKS: lambda: (pack.at[both], pack.at[past]),
            F1_TOP: lambda: at(F1, 1), F1_LOW: lambda: at(F1, rows), F1_MID: lambda: at(F1, mid),
            F0_TOP: lambda: at(F0, 1), F0_LOW: lambda: at(F0, rows), F0_MID: lambda: at(F0, mid),
            H1_HALO: lambda: (halo.at[H1 - 4, 0], halo.at[H1P - 4, 0]),
            H1_IN: lambda: at(H1, body, inner), H1_LEFT: lambda: at(H1, body, left), H1_RIGHT: lambda: at(H1, body, right),
            H0_HALO: lambda: (halo.at[H0 - 4, 0], halo.at[H0P - 4, 0]),
            H0_TOP: lambda: at(H0, 1), H0_LOW: lambda: at(H0, rows), H0_MID: lambda: at(H0, mid),
        }[i]()
        return remote(src, dst, (zsend, zrecv), i, {"tm": lax.rem(tm + 1, groups)})

    def send_on(*parts):
        pl.when(has_next)(lambda: [forward(p).start() for p in parts] and None)

    def arrived(*parts):
        pl.when(has_prev)(lambda: [forward(p).wait_recv() for p in parts] and None)

    def own(d):
        if d in RIM:
            src, dst = pack.at[both, int(STEP[d][0] > 0)], rim.at[both, RIM[d]]
        else:
            src, dst = xc.at[both, 1 if d == U else rows], xc.at[both, rows + 1 if d == U else 0]
        return remote(src, dst, (lsend, lrecv), d, device(d))

    def past_pack(d):
        return remote(pack.at[past, int(STEP[d][0] > 0)], rim.at[past, RIM[d]], (lsend, lrecv), 8 + d, device(d))

    def row(s):
        base = {F1P: 8, F0P: 16}.get(s, 24 + 4 * (s - 4))

        def make(d):
            return remote(
                xc.at[s, 1 if d == U else rows], xc.at[s, rows + 1 if d == U else 0],
                (lsend, lrecv), base + (d if s < H0P else int(d == D)), device(d))
        return make

    def halo_of(s):
        def make(d):
            return remote(
                halo.at[s - 4, 0], halo.at[s - 4, 2 if d == U else 1],
                (lsend, lrecv), 26 + 4 * (s - 4) + int(d == D), device(d))
        return make

    def send(*makes):
        return [lambda d, make=make: make(d).start() for make in makes]

    def receive(*makes):
        return [lambda d, make=make: make(BACK[d]).wait_recv() for make in makes]

    def sent(*makes):
        return [lambda d, make=make: make(d).wait_send() for make in makes]

    def if_past(run):
        pl.when(has_prev)(run)

    ROWS, SIDES = (U, D), (E, UE, DE, W, UW, DW)

    @pl.when(jnp.logical_not(has_prev))
    def _():
        for s in (F0P, F1P, H0P, H1P):
            xc[s] = jnp.zeros(xc.shape[1:], BF16)
        pack[past] = jnp.zeros((2, *pack.shape[1:]), BF16)
        rim[past] = jnp.zeros((2, *rim.shape[1:]), BF16)
        halo[0:2] = jnp.zeros((2, *halo.shape[1:]), BF16)

    @pl.when(jnp.logical_not(has_up))
    def _():
        for s in range(8):
            xc[s, 0] = jnp.zeros((cols, chan), BF16)
        for s in range(4):
            rim[s, 2:4] = jnp.zeros((2, 2 * rows, chan), BF16)
            halo[s, 1] = jnp.zeros((2 * rows, chan), BF16)

    @pl.when(jnp.logical_not(has_down))
    def _():
        for s in range(8):
            xc[s, rows + 1] = jnp.zeros((cols, chan), BF16)
        for s in range(4):
            rim[s, 4:6] = jnp.zeros((2, 2 * rows, chan), BF16)
            halo[s, 2] = jnp.zeros((2 * rows, chan), BF16)

    def make_pack(s):
        for half, at in ((0, 0), (1, cols - T)):
            tile = [xc[s, r, at:at + T] for r in range(1, rows + 1)]
            js = (0, 1) if half == 0 else (T - 2, T - 1)
            pack[s, half] = jnp.concatenate([x[j:j + 1] for j in js for x in tile], axis=0)

    def beside(s, r):
        if s < H0P:
            if r == 0:
                return rim[s, 2, 2 * rows - 1:], rim[s, 3, rows - 1:rows]
            if r == rows + 1:
                return rim[s, 4, rows:rows + 1], rim[s, 5, 0:1]
            return rim[s, 0, rows + r - 1:rows + r], rim[s, 1, r - 1:r]
        if r == 0:
            return halo[s - 4, 1, rows - 1:rows], halo[s - 4, 1, 2 * rows - 1:]
        if r == rows + 1:
            return halo[s - 4, 2, 0:1], halo[s - 4, 2, rows:rows + 1]
        return halo[s - 4, 0, r - 1:r], halo[s - 4, 0, rows + r - 1:rows + r]

    def shift_in(s):
        for r in range(rows + 2):
            x = xc[s, r]
            xl[s, r, T:cols - T] = x[T - 1:cols - T - 1]
            xr[s, r, T:cols - T] = x[T + 1:cols - T + 1]

    def shift_out(s):
        for r in range(rows + 2):
            before, after = beside(s, r)
            x = xc[s, r]
            xl[s, r, 0:T] = jnp.concatenate([before, x[:T - 1]], axis=0)
            xl[s, r, cols - T:] = x[cols - T - 1:cols - 1]
            xr[s, r, 0:T] = x[1:T + 1]
            xr[s, r, cols - T:] = jnp.concatenate([x[cols - T + 1:], after], axis=0)

    def shift_all(s):
        for r in range(rows + 2):
            before, after = beside(s, r)
            x = xc[s, r]
            xl[s, r] = jnp.concatenate([before, x[:cols - 1]], axis=0)
            xr[s, r] = jnp.concatenate([x[1:], after], axis=0)

    def halo_taps(s):
        def column(above, mid, below):
            above, mid, below = above.astype(F32), mid.astype(F32), below.astype(F32)
            return (jnp.concatenate([above, mid[:rows - 1]], axis=0), mid, jnp.concatenate([mid[1:], below], axis=0))

        def rim_column(at, side):
            k = side
            return column(rim[s, k + 2, at + rows - 1:at + rows], rim[s, k, at:at + rows], rim[s, k + 4, at:at + 1])

        first = column(xc[s, 0, 0:1], pack[s, 0, 0:rows], xc[s, rows + 1, 0:1])
        last = column(xc[s, 0, cols - 1:], pack[s, 1, rows:], xc[s, rows + 1, cols - 1:])
        wests = (rim_column(0, 0), rim_column(rows, 0), first)
        easts = (last, rim_column(0, 1), rim_column(rows, 1))
        return jnp.concatenate(
            [jnp.concatenate([wests[c][b], easts[c][b]], axis=0).astype(BF16) for b in range(3) for c in range(3)], axis=1)

    IN, OUT, ALL = (slice(T, cols - T),), (slice(0, T), slice(cols - T, cols)), (slice(0, cols),)

    def taken(ref, s, b, cuts):
        some = [ref[s, b:b + rows, c] for c in cuts]
        some = some[0] if len(some) == 1 else jnp.concatenate(some, axis=1)
        return some.reshape(-1, chan)

    def taps(s, w, times, cuts):
        x = jnp.concatenate([taken(ref, s, b, cuts) for b in range(3) for ref in (xl, xc, xr)], axis=1)
        if cuts is OUT:
            x = jnp.concatenate([x, halo_taps(s)], axis=0)
        k = jnp.concatenate([w[a].reshape(9 * chan, chan) for a in times], axis=1)
        return jnp.dot(x, k, preferred_element_type=F32)

    def shift(s, cuts):
        (shift_in if cuts is IN else shift_out if cuts is OUT else shift_all)(s)

    def own_later(s, w, acc, cuts):
        shift(s, cuts)
        acc[:, chan:] = taps(s, w, (2,), cuts)

    def own_earlier(s, w, acc, cuts):
        shift(s, cuts)
        v = taps(s, w, (2, 1), cuts)
        acc[:, :chan] = v[:, :chan]
        acc[:, chan:] += v[:, chan:]

    def past_later(s, w, acc, cuts):
        shift(s, cuts)
        v = acc[...] + taps(s, w, (1, 0), cuts)
        acc[:, :chan] = v[:, :chan]
        return v[:, chan:]

    def past_earlier(s, w, acc, cuts):
        shift(s, cuts)
        return acc[:, :chan] + taps(s, w, (0,), cuts)

    def silu(v):
        return (v / (1 + jnp.exp(-v))).astype(BF16)

    def hidden_in(s, v):
        xc[s, 1:rows + 1, T:cols - T] = silu(v).reshape(rows, cols - 2 * T, chan)

    def hidden_out(s, v):
        h = silu(v)
        halo[s - 4, 0] = h[2 * T * rows:]
        h = h[:2 * T * rows].reshape(rows, 2 * T, chan)
        xc[s, 1:rows + 1, 0:T] = h[:, :T]
        xc[s, 1:rows + 1, cols - T:] = h[:, T:]

    def result(t, v):
        x = xc[(F0, F1)[t], 1:rows + 1].reshape(-1, chan).astype(F32) + v
        o_ref[t] = x.astype(BF16).reshape(rows, cols, chan)

    for s, copy in ((F1, loads[0]), (F0, loads[1])):
        copy.wait()
        make_pack(s)

    def count(d):
        there = (has_up, True, has_down)[STEP[d][1] + 1]
        return (greets_me(d) if there is True else jnp.logical_and(there, greets_me(d))).astype(I32)

    pl.semaphore_wait(barrier, has_next.astype(I32) + sum(count(d) for d in range(8)))

    send_on(PACKS, F1_TOP, F1_LOW, F1_MID, F0_TOP, F0_LOW, F0_MID)

    def tell(d):
        pl.semaphore_signal(entered.at[BACK[d]], inc=1, device_id=device(d), device_id_type=MESH)

    def told(d):
        pl.semaphore_wait(entered.at[d], 1)

    toward_if(lambda d: jnp.logical_not(i_greet(d)), range(8), tell)

    def known(ds, *runs):
        toward(ds, lambda d: pl.when(greets_me(d))(lambda: [run(d) for run in runs] and None))

    def late(d):
        far = jnp.logical_and(lon == 0, STEP[d][0] < 0)
        return far if d in (D, DE, DW) else jnp.logical_or(far, to_origin(d))

    def soon(d):
        return jnp.logical_not(jnp.logical_or(greets_me(d), late(d)))

    def last(d):
        return jnp.logical_and(jnp.logical_not(greets_me(d)), late(d))

    def send_past_pack(d):
        if_past(lambda: past_pack(d).start())

    def after_word(cond):
        def run(d):
            told(d)
            own(d).start()
            if d in RIM:
                send_past_pack(d)
        toward(ROWS + SIDES, lambda d: pl.when(cond(d))(lambda: run(d)))

    known(ROWS + SIDES, *send(own))
    arrived(PACKS)
    if_past(lambda: known(SIDES, *send(past_pack)))
    arrived(F1_TOP, F1_LOW)
    if_past(lambda: toward(ROWS, *send(row(F1P))))
    loads[2].wait()
    toward(ROWS, *receive(own))
    own_later(F1, w1, acc_in, IN)
    own_earlier(F0, w1, acc_in, IN)
    after_word(soon)
    arrived(F1_MID)
    if_past(lambda: toward(ROWS, *receive(row(F1P))))
    hidden_in(H1, past_later(F1P, w1, acc_in, IN))
    send_on(H1_IN)
    arrived(F0_TOP, F0_LOW)
    if_past(lambda: toward(ROWS, *send(row(F0P))))
    after_word(last)

    toward(SIDES, *receive(own))
    own_later(F1, w1, acc_out, OUT)
    own_earlier(F0, w1, acc_out, OUT)
    if_past(lambda: toward(SIDES, *receive(past_pack)))
    hidden_out(H1, past_later(F1P, w1, acc_out, OUT))
    send_on(H1_HALO, H1_LEFT, H1_RIGHT)
    toward(ROWS, *send(row(H1), halo_of(H1)))
    arrived(F0_MID)
    if_past(lambda: toward(ROWS, *receive(row(F0P))))
    hidden_in(H0, past_earlier(F0P, w1, acc_in, IN))
    hidden_out(H0, past_earlier(F0P, w1, acc_out, OUT))
    send_on(H0_HALO, H0_TOP, H0_LOW, H0_MID)
    toward(ROWS, *send(row(H0), halo_of(H0)))

    loads[3].wait()
    pl.when(has_next)(lambda: [forward(p).wait_send() for p in range(H1_HALO)] and None)
    toward(ROWS + SIDES, *sent(own))

    @pl.when(has_prev)
    def _():
        toward(SIDES, *sent(past_pack))
        toward(ROWS, *sent(row(F1P), row(F0P)))

    toward(ROWS, *receive(row(H1), halo_of(H1)))
    own_later(H1, w2, acc, ALL)
    arrived(H1_HALO, H1_IN, H1_LEFT, H1_RIGHT)
    if_past(lambda: toward(ROWS, *send(row(H1P), halo_of(H1P))))
    arrived(H0_HALO, H0_TOP, H0_LOW)
    if_past(lambda: toward(ROWS, *send(row(H0P), halo_of(H0P))))
    toward(ROWS, *receive(row(H0), halo_of(H0)))
    own_earlier(H0, w2, acc, ALL)
    pl.when(has_next)(lambda: [forward(p).wait_send() for p in range(H1_HALO, 15)] and None)
    toward(ROWS, *sent(row(H0), halo_of(H0), row(H1), halo_of(H1)))
    if_past(lambda: toward(ROWS, *receive(row(H1P), halo_of(H1P))))
    result(1, past_later(H1P, w2, acc, ALL))
    arrived(H0_MID)
    if_past(lambda: toward(ROWS, *receive(row(H0P), halo_of(H0P))))
    result(0, past_earlier(H0P, w2, acc, ALL))
    if_past(lambda: toward(ROWS, *sent(row(H1P), halo_of(H1P), row(H0P), halo_of(H0P))))


def solution(mesh):
    groups, tiles_lon, tiles_lat = mesh.shape["tm"], mesh.shape["lon"], mesh.shape["lat"]

    def local(features, conv_first, conv_second):
        frames, rows, cols, chan = features.shape
        frame = (8, rows + 2, cols, chan)
        outer = 2 * T * rows + 2 * rows

        def kernel(*refs):
            block(groups, tiles_lon, tiles_lat, *refs)

        return pl.pallas_call(
            kernel,
            out_shape=pltpu.VMEM(features.shape, BF16),
            in_specs=[pl.BlockSpec(memory_space=pltpu.HBM)] * 3,
            out_specs=pl.BlockSpec(memory_space=pltpu.VMEM),
            scratch_shapes=[
                pltpu.VMEM(frame, BF16),
                pltpu.VMEM(frame, BF16),
                pltpu.VMEM(frame, BF16),
                pltpu.VMEM((4, 2, 2 * rows, chan), BF16),
                pltpu.VMEM((4, 6, 2 * rows, chan), BF16),
                pltpu.VMEM((4, 3, 2 * rows, chan), BF16),
                pltpu.VMEM(conv_first.shape, BF16),
                pltpu.VMEM(conv_second.shape, BF16),
                pltpu.VMEM(((cols - 2 * T) * rows, 2 * chan), F32),
                pltpu.VMEM((outer, 2 * chan), F32),
                pltpu.VMEM((rows * cols, 2 * chan), F32),
                pltpu.SemaphoreType.DMA((15,)),
                pltpu.SemaphoreType.DMA((15,)),
                pltpu.SemaphoreType.DMA((40,)),
                pltpu.SemaphoreType.DMA((40,)),
                pltpu.SemaphoreType.DMA((4,)),
                pltpu.SemaphoreType.REGULAR((8,)),
            ],
            compiler_params=pltpu.CompilerParams(
                collective_id=0, has_side_effects=True, vmem_limit_bytes=32 * 2**20),
            cost_estimate=pl.CostEstimate(
                flops=4 * frames * rows * cols * 27 * chan * chan, bytes_accessed=3 * 2**20, transcendentals=2**17),
            name="conv_block",
        )(*(pltpu.with_memory_space_constraint(x, pltpu.HBM) for x in (features, conv_first, conv_second)))

    placed = P("tm", "lat", "lon", None)
    return jax.shard_map(local, mesh=mesh, in_specs=(placed, P(), P()), out_specs=placed, check_vma=False)
```

```python
import jax
import jax.numpy as jnp
from jax import lax
from jax.experimental import pallas as pl
from jax.experimental.pallas import tpu as pltpu
from jax.sharding import PartitionSpec as P

MESH = pl.DeviceIdType.MESH
BF16, F32, I32 = jnp.bfloat16, jnp.float32, jnp.int32
F0P, F1P, F0, F1, H0P, H1P, H0, H1 = range(8)
NEXT = {F0: F0P, F1: F1P, H0: H0P, H1: H1P}
E, W, U, UE, UW, D, DE, DW = range(8)
STEP = {E: (1, 0), W: (-1, 0), U: (0, -1), UE: (1, -1), UW: (-1, -1), D: (0, 1), DE: (1, 1), DW: (-1, 1)}
BACK = {E: W, W: E, U: D, D: U, UE: DW, DW: UE, UW: DE, DE: UW}
RIM = {E: 0, W: 1, DE: 2, DW: 3, UE: 4, UW: 5}
T = 16


def block(groups, tiles_lon, tiles_lat, f_ref, k1_ref, k2_ref, o_ref, xc, xl, xr, pack, rim, halo, w1, w2,
          acc_in, acc_out, acc, zsend, zrecv, lsend, lrecv, load, entered):
    tm, lon, lat = lax.axis_index("tm"), lax.axis_index("lon"), lax.axis_index("lat")
    rows, cols, chan = f_ref.shape[1:]
    has_prev, has_next, has_up, has_down = tm > 0, tm < groups - 1, lat > 0, lat < tiles_lat - 1

    ring = tiles_lon // 2

    def lateness(at):
        y = lax.rem(at, ring)
        return jnp.minimum(y, ring - y)

    east, west = lax.rem(lon + 1, tiles_lon), lax.rem(lon + tiles_lon - 1, tiles_lon)
    earlier_e, earlier_w = lateness(east) < lateness(lon), lateness(west) < lateness(lon)
    later_e, later_w = jnp.logical_not(earlier_e), jnp.logical_not(earlier_w)
    far_e, far_w = lax.rem(lon, ring) == ring - 1, lax.rem(lon, ring) == 0
    near_e, near_w = jnp.logical_not(far_e), jnp.logical_not(far_w)
    up, down = lax.rem(lat + tiles_lat - 1, tiles_lat), lax.rem(lat + 1, tiles_lat)

    def device(d):
        step_lon, step_lat = STEP[d]
        to = {}
        if step_lon:
            to["lon"] = east if step_lon > 0 else west
        if step_lat:
            to["lat"] = down if step_lat > 0 else up
        return to

    def toward(ds, *runs):
        def some(rise):
            return [d for d in ds if STEP[d][1] == rise]

        def all_of(ds):
            for run in runs:
                for d in ds:
                    run(d)

        all_of(some(0))
        for rise, cond in ((-1, has_up), (1, has_down)):
            if some(rise):
                pl.when(cond)(lambda rise=rise: all_of(some(rise)))

    barrier = pltpu.get_barrier_semaphore()

    def greet(d):
        pl.semaphore_signal(barrier, inc=1, device_id=device(d), device_id_type=MESH)

    @pl.when(has_prev)
    def _():
        pl.semaphore_signal(barrier, inc=1, device_id={"tm": tm - 1}, device_id_type=MESH)

    origin = jnp.logical_and(tm == 0, jnp.logical_and(lon == 0, lat == 0))
    awake = jnp.logical_not(origin)
    lon_of, lat_of = {0: lon, 1: east, -1: west}, {0: lat, 1: down, -1: up}

    def to_origin(d):
        x, y = STEP[d]
        return jnp.logical_and(tm == 0, jnp.logical_and(lon_of[x] == 0, lat_of[y] == 0))

    def either(a, b):
        return True if a is True or b is True else jnp.logical_or(a, b)

    def greets_me(d):
        first = {U: True, D: True, E: either(near_e, earlier_e), W: near_w}.get(d, earlier_e if STEP[d][0] > 0 else earlier_w)
        if d in (D, DE, DW):
            return either(origin, first)
        return jnp.logical_and(either(origin, first), jnp.logical_not(to_origin(d)))

    def i_greet(d):
        first = {U: True, D: True, E: near_e, W: True}.get(d, later_e if STEP[d][0] > 0 else later_w)
        if d in (D, DE, DW):
            return jnp.logical_and(awake, first)
        return jnp.logical_and(awake, either(first, to_origin(d)))

    def toward_if(cond, ds, *runs):
        toward(ds, *[lambda d, run=run: pl.when(cond(d))(lambda: run(d)) for run in runs])

    toward_if(i_greet, range(8), greet)

    EAST, WEST = (E, UE, DE), (W, UW, DW)
    from_last, to_first = jnp.logical_and(lon == 0, has_prev), jnp.logical_and(lon == tiles_lon - 1, has_next)

    @pl.when(from_last)
    def _():
        toward(WEST, lambda d: pl.semaphore_signal(
            barrier, inc=1, device_id={"tm": tm - 1, **device(d)}, device_id_type=MESH))


    loads = [
        pltpu.make_async_copy(f_ref.at[1], xc.at[F1, pl.ds(1, rows)], load.at[0]),
        pltpu.make_async_copy(f_ref.at[0], xc.at[F0, pl.ds(1, rows)], load.at[1]),
        pltpu.make_async_copy(k1_ref, w1, load.at[2]),
        pltpu.make_async_copy(k2_ref, w2, load.at[3]),
    ]
    for copy in loads:
        copy.start()

    def remote(src, dst, sems, i, to):
        return pltpu.make_async_remote_copy(
            src_ref=src, dst_ref=dst, send_sem=sems[0].at[i], recv_sem=sems[1].at[i], device_id=to, device_id_type=MESH)

    both, past = pl.ds(F0, 2), pl.ds(F0P, 2)
    left, inner, right = pl.ds(0, T), pl.ds(T, cols - 2 * T), pl.ds(cols - T, T)

    PACKS, F1_TOP, F1_LOW, F1_MID, F0_TOP, F0_LOW, F0_MID = range(7)
    H1_HALO, H1_IN, H1_TOP, H1_LOW, H1_LEFT, H1_RIGHT, H0_HALO, H0_TOP, H0_LOW, H0_MID = range(7, 17)

    def forward(i):
        def at(s, *where):
            return xc.at[(s, *where)], xc.at[(NEXT[s], *where)]

        mid = pl.ds(2, rows - 2)
        src, dst = {
            PACKS: lambda: (pack.at[both], pack.at[past]),
            F1_TOP: lambda: at(F1, 1), F1_LOW: lambda: at(F1, rows), F1_MID: lambda: at(F1, mid),
            F0_TOP: lambda: at(F0, 1), F0_LOW: lambda: at(F0, rows), F0_MID: lambda: at(F0, mid),
            H1_HALO: lambda: (halo.at[H1 - 4, 0], halo.at[H1P - 4, 0]),
            H1_IN: lambda: at(H1, mid, inner), H1_TOP: lambda: at(H1, 1), H1_LOW: lambda: at(H1, rows),
            H1_LEFT: lambda: at(H1, mid, left), H1_RIGHT: lambda: at(H1, mid, right),
            H0_HALO: lambda: (halo.at[H0 - 4, 0], halo.at[H0P - 4, 0]),
            H0_TOP: lambda: at(H0, 1), H0_LOW: lambda: at(H0, rows), H0_MID: lambda: at(H0, mid),
        }[i]()
        return remote(src, dst, (zsend, zrecv), i, {"tm": lax.rem(tm + 1, groups)})

    def send_on(*parts):
        pl.when(has_next)(lambda: [forward(p).start() for p in parts] and None)

    def arrived(*parts):
        pl.when(has_prev)(lambda: [forward(p).wait_recv() for p in parts] and None)

    def own(d):
        if d in RIM:
            src, dst = pack.at[both, int(STEP[d][0] > 0)], rim.at[both, RIM[d]]
        else:
            src, dst = xc.at[both, 1 if d == U else rows], xc.at[both, rows + 1 if d == U else 0]
        return remote(src, dst, (lsend, lrecv), d, device(d))

    def past_pack(d):
        return remote(pack.at[past, int(STEP[d][0] > 0)], rim.at[past, RIM[d]], (lsend, lrecv), 8 + d, device(d))

    def direct_pack(d):
        return remote(
            pack.at[both, 1], rim.at[past, RIM[d]], (lsend, lrecv), 8 + d, {"tm": lax.rem(tm + 1, groups), **device(d)})

    def row(s):
        base = {F1P: 8, F0P: 16}.get(s, 24 + 4 * (s - 4))

        def make(d):
            return remote(
                xc.at[s, 1 if d == U else rows], xc.at[s, rows + 1 if d == U else 0],
                (lsend, lrecv), base + (d if s < H0P else int(d == D)), device(d))
        return make

    def halo_of(s):
        def make(d):
            return remote(
                halo.at[s - 4, 0], halo.at[s - 4, 2 if d == U else 1],
                (lsend, lrecv), 26 + 4 * (s - 4) + int(d == D), device(d))
        return make

    def send(*makes):
        return [lambda d, make=make: make(d).start() for make in makes]

    def receive(*makes):
        return [lambda d, make=make: make(BACK[d]).wait_recv() for make in makes]

    def sent(*makes):
        return [lambda d, make=make: make(d).wait_send() for make in makes]

    def if_past(run):
        pl.when(has_prev)(run)

    ROWS, SIDES = (U, D), (E, UE, DE, W, UW, DW)

    @pl.when(jnp.logical_not(has_prev))
    def _():
        for s in (F0P, F1P, H0P, H1P):
            xc[s] = jnp.zeros(xc.shape[1:], BF16)
        pack[past] = jnp.zeros((2, *pack.shape[1:]), BF16)
        rim[past] = jnp.zeros((2, *rim.shape[1:]), BF16)
        halo[0:2] = jnp.zeros((2, *halo.shape[1:]), BF16)

    @pl.when(jnp.logical_not(has_up))
    def _():
        for s in range(8):
            xc[s, 0] = jnp.zeros((cols, chan), BF16)
        for s in range(4):
            rim[s, 2:4] = jnp.zeros((2, 2 * rows, chan), BF16)
            halo[s, 1] = jnp.zeros((2 * rows, chan), BF16)

    @pl.when(jnp.logical_not(has_down))
    def _():
        for s in range(8):
            xc[s, rows + 1] = jnp.zeros((cols, chan), BF16)
        for s in range(4):
            rim[s, 4:6] = jnp.zeros((2, 2 * rows, chan), BF16)
            halo[s, 2] = jnp.zeros((2 * rows, chan), BF16)

    def make_pack(s):
        for half, at in ((0, 0), (1, cols - T)):
            tile = [xc[s, r, at:at + T] for r in range(1, rows + 1)]
            js = (0, 1) if half == 0 else (T - 2, T - 1)
            pack[s, half] = jnp.concatenate([x[j:j + 1] for j in js for x in tile], axis=0)

    def beside(s, r):
        if s < H0P:
            if r == 0:
                return rim[s, 2, 2 * rows - 1:], rim[s, 3, rows - 1:rows]
            if r == rows + 1:
                return rim[s, 4, rows:rows + 1], rim[s, 5, 0:1]
            return rim[s, 0, rows + r - 1:rows + r], rim[s, 1, r - 1:r]
        if r == 0:
            return halo[s - 4, 1, rows - 1:rows], halo[s - 4, 1, 2 * rows - 1:]
        if r == rows + 1:
            return halo[s - 4, 2, 0:1], halo[s - 4, 2, rows:rows + 1]
        return halo[s - 4, 0, r - 1:r], halo[s - 4, 0, rows + r - 1:rows + r]

    def shift_in(s):
        for r in range(1, rows + 1):
            x = xc[s, r]
            xl[s, r, T:cols - T] = x[T - 1:cols - T - 1]
            xr[s, r, T:cols - T] = x[T + 1:cols - T + 1]

    def shift_out(s):
        for r in range(rows + 2):
            before, after = beside(s, r)
            x = xc[s, r]
            if r in (0, rows + 1):
                xl[s, r, T:cols - T] = x[T - 1:cols - T - 1]
                xr[s, r, T:cols - T] = x[T + 1:cols - T + 1]
            xl[s, r, 0:T] = jnp.concatenate([before, x[:T - 1]], axis=0)
            xl[s, r, cols - T:] = x[cols - T - 1:cols - 1]
            xr[s, r, 0:T] = x[1:T + 1]
            xr[s, r, cols - T:] = jnp.concatenate([x[cols - T + 1:], after], axis=0)

    def shift_all(s):
        for r in range(rows + 2):
            before, after = beside(s, r)
            x = xc[s, r]
            xl[s, r] = jnp.concatenate([before, x[:cols - 1]], axis=0)
            xr[s, r] = jnp.concatenate([x[1:], after], axis=0)

    def halo_taps(s):
        def column(above, mid, below):
            above, mid, below = above.astype(F32), mid.astype(F32), below.astype(F32)
            return (jnp.concatenate([above, mid[:rows - 1]], axis=0), mid, jnp.concatenate([mid[1:], below], axis=0))

        def rim_column(at, side):
            k = side
            return column(rim[s, k + 2, at + rows - 1:at + rows], rim[s, k, at:at + rows], rim[s, k + 4, at:at + 1])

        first = column(xc[s, 0, 0:1], pack[s, 0, 0:rows], xc[s, rows + 1, 0:1])
        last = column(xc[s, 0, cols - 1:], pack[s, 1, rows:], xc[s, rows + 1, cols - 1:])
        wests = (rim_column(0, 0), rim_column(rows, 0), first)
        easts = (last, rim_column(0, 1), rim_column(rows, 1))
        return jnp.concatenate(
            [jnp.concatenate([wests[c][b], easts[c][b]], axis=0).astype(BF16) for b in range(3) for c in range(3)], axis=1)

    MID, INNER = slice(1, rows - 1), slice(T, cols - T)
    IN = ((MID, INNER),)
    OUT = ((slice(0, rows), slice(0, T)), (slice(0, rows), slice(cols - T, cols)), (slice(0, 1), INNER), (slice(rows - 1, rows), INNER))
    ALL = ((slice(0, rows), slice(0, cols)),)

    def taken(ref, s, b, cuts):
        some = [ref[s, r.start + b:r.stop + b, c].reshape(-1, chan) for r, c in cuts]
        return some[0] if len(some) == 1 else jnp.concatenate(some, axis=0)

    def taps(s, w, times, cuts):
        x = jnp.concatenate([taken(ref, s, b, cuts) for b in range(3) for ref in (xl, xc, xr)], axis=1)
        if cuts is OUT:
            x = jnp.concatenate([x, halo_taps(s)], axis=0)
        k = jnp.concatenate([w[a].reshape(9 * chan, chan) for a in times], axis=1)
        return jnp.dot(x, k, preferred_element_type=F32)

    def shift(s, cuts):
        (shift_in if cuts is IN else shift_out if cuts is OUT else shift_all)(s)

    def own_later(s, w, acc, cuts):
        shift(s, cuts)
        acc[:, chan:] = taps(s, w, (2,), cuts)

    def own_earlier(s, w, acc, cuts):
        shift(s, cuts)
        v = taps(s, w, (2, 1), cuts)
        acc[:, :chan] = v[:, :chan]
        acc[:, chan:] += v[:, chan:]

    def past_later(s, w, acc, cuts):
        shift(s, cuts)
        v = acc[...] + taps(s, w, (1, 0), cuts)
        acc[:, :chan] = v[:, :chan]
        return v[:, chan:]

    def past_earlier(s, w, acc, cuts):
        shift(s, cuts)
        return acc[:, :chan] + taps(s, w, (0,), cuts)

    def silu(v):
        return (v / (1 + jnp.exp(-v))).astype(BF16)

    def hidden_part(s, h, cuts):
        at = 0
        for r, c in cuts:
            high, wide = r.stop - r.start, c.stop - c.start
            xc[s, r.start + 1:r.stop + 1, c] = h[at:at + high * wide].reshape(high, wide, chan)
            at += high * wide
        return at

    def hidden_in(s, v):
        hidden_part(s, silu(v), IN)

    def hidden_out(s, v):
        h = silu(v)
        at = hidden_part(s, h, OUT)
        halo[s - 4, 0] = h[at:]

    def result(t, v):
        x = xc[(F0, F1)[t], 1:rows + 1].reshape(-1, chan).astype(F32) + v
        o_ref[t] = x.astype(BF16).reshape(rows, cols, chan)

    for s, copy in ((F1, loads[0]), (F0, loads[1])):
        copy.wait()
        make_pack(s)

    def count(d):
        there = (has_up, True, has_down)[STEP[d][1] + 1]
        return (greets_me(d) if there is True else jnp.logical_and(there, greets_me(d))).astype(I32)

    pl.semaphore_wait(
        barrier, has_next.astype(I32) + sum(count(d) for d in range(8))
        + to_first.astype(I32) * (1 + has_up.astype(I32) + has_down.astype(I32)))

    send_on(PACKS)
    pl.when(to_first)(lambda: toward(EAST, *send(direct_pack)))
    send_on(F1_TOP, F1_LOW, F1_MID, F0_TOP, F0_LOW, F0_MID)

    def tell(d):
        pl.semaphore_signal(entered.at[BACK[d]], inc=1, device_id=device(d), device_id_type=MESH)

    def told(d):
        pl.semaphore_wait(entered.at[d], 1)

    toward_if(lambda d: jnp.logical_not(i_greet(d)), range(8), tell)

    def known(ds, *runs):
        toward(ds, lambda d: pl.when(greets_me(d))(lambda: [run(d) for run in runs] and None))

    def late(d):
        far = jnp.logical_and(lon == 0, STEP[d][0] < 0)
        return far if d in (D, DE, DW) else jnp.logical_or(far, to_origin(d))

    def soon(d):
        return jnp.logical_not(jnp.logical_or(greets_me(d), late(d)))

    def last(d):
        return jnp.logical_and(jnp.logical_not(greets_me(d)), late(d))

    def send_past_pack(d):
        if d in EAST:
            pl.when(jnp.logical_and(has_prev, inland))(lambda: past_pack(d).start())
        else:
            if_past(lambda: past_pack(d).start())

    def after_word(cond):
        def run(d):
            told(d)
            own(d).start()
            if d in RIM:
                send_past_pack(d)
        toward(ROWS + SIDES, lambda d: pl.when(cond(d))(lambda: run(d)))

    known(ROWS + SIDES, *send(own))
    loads[2].wait()
    own_later(F1, w1, acc_in, IN)
    own_earlier(F0, w1, acc_in, IN)
    arrived(PACKS)
    if_past(lambda: known(WEST, *send(past_pack)))
    inland = lon < tiles_lon - 1
    pl.when(jnp.logical_and(has_prev, inland))(lambda: known(EAST, *send(past_pack)))
    arrived(F1_TOP, F1_LOW)
    if_past(lambda: toward(ROWS, *send(row(F1P))))
    after_word(soon)
    arrived(F1_MID)
    hidden_in(H1, past_later(F1P, w1, acc_in, IN))
    send_on(H1_IN)
    arrived(F0_TOP, F0_LOW)
    if_past(lambda: toward(ROWS, *send(row(F0P))))
    after_word(last)

    toward(ROWS + SIDES, *receive(own))
    own_later(F1, w1, acc_out, OUT)
    own_earlier(F0, w1, acc_out, OUT)

    def inner_earlier():
        arrived(F0_MID)
        hidden_in(H0, past_earlier(F0P, w1, acc_in, IN))

    far = jnp.logical_or(far_e, far_w)
    pl.when(far)(inner_earlier)
    if_past(lambda: toward(SIDES, *receive(past_pack)))
    if_past(lambda: toward(ROWS, *receive(row(F1P))))
    hidden_out(H1, past_later(F1P, w1, acc_out, OUT))
    send_on(H1_HALO, H1_TOP, H1_LOW, H1_LEFT, H1_RIGHT)
    toward(ROWS, *send(row(H1), halo_of(H1)))
    pl.when(jnp.logical_not(far))(inner_earlier)
    if_past(lambda: toward(ROWS, *receive(row(F0P))))
    hidden_out(H0, past_earlier(F0P, w1, acc_out, OUT))
    send_on(H0_HALO, H0_TOP, H0_LOW, H0_MID)
    toward(ROWS, *send(row(H0), halo_of(H0)))

    loads[3].wait()
    pl.when(has_next)(lambda: [forward(p).wait_send() for p in range(H1_HALO)] and None)
    toward(ROWS + SIDES, *sent(own))
    pl.when(to_first)(lambda: toward(EAST, *sent(direct_pack)))

    @pl.when(has_prev)
    def _():
        toward(WEST, *sent(past_pack))
        pl.when(inland)(lambda: toward(EAST, *sent(past_pack)))
        toward(ROWS, *sent(row(F1P), row(F0P)))

    arrived(H1_HALO, H1_TOP, H1_LOW)
    if_past(lambda: toward(ROWS, *send(row(H1P), halo_of(H1P))))
    toward(ROWS, *receive(row(H1), halo_of(H1)))
    own_later(H1, w2, acc, ALL)
    arrived(H0_HALO, H0_TOP, H0_LOW)
    if_past(lambda: toward(ROWS, *send(row(H0P), halo_of(H0P))))
    toward(ROWS, *receive(row(H0), halo_of(H0)))
    own_earlier(H0, w2, acc, ALL)
    pl.when(has_next)(lambda: [forward(p).wait_send() for p in range(H1_HALO, 17)] and None)
    toward(ROWS, *sent(row(H0), halo_of(H0), row(H1), halo_of(H1)))
    if_past(lambda: toward(ROWS, *receive(row(H1P), halo_of(H1P))))
    arrived(H1_IN, H1_LEFT, H1_RIGHT)
    result(1, past_later(H1P, w2, acc, ALL))
    arrived(H0_MID)
    if_past(lambda: toward(ROWS, *receive(row(H0P), halo_of(H0P))))
    result(0, past_earlier(H0P, w2, acc, ALL))
    if_past(lambda: toward(ROWS, *sent(row(H1P), halo_of(H1P), row(H0P), halo_of(H0P))))


def solution(mesh):
    groups, tiles_lon, tiles_lat = mesh.shape["tm"], mesh.shape["lon"], mesh.shape["lat"]

    def local(features, conv_first, conv_second):
        frames, rows, cols, chan = features.shape
        frame = (8, rows + 2, cols, chan)
        inner = (cols - 2 * T) * (rows - 2)
        outer = rows * cols - inner + 2 * rows

        def kernel(*refs):
            block(groups, tiles_lon, tiles_lat, *refs)

        return pl.pallas_call(
            kernel,
            out_shape=pltpu.VMEM(features.shape, BF16),
            in_specs=[pl.BlockSpec(memory_space=pltpu.HBM)] * 3,
            out_specs=pl.BlockSpec(memory_space=pltpu.VMEM),
            scratch_shapes=[
                pltpu.VMEM(frame, BF16),
                pltpu.VMEM(frame, BF16),
                pltpu.VMEM(frame, BF16),
                pltpu.VMEM((4, 2, 2 * rows, chan), BF16),
                pltpu.VMEM((4, 6, 2 * rows, chan), BF16),
                pltpu.VMEM((4, 3, 2 * rows, chan), BF16),
                pltpu.VMEM(conv_first.shape, BF16),
                pltpu.VMEM(conv_second.shape, BF16),
                pltpu.VMEM((inner, 2 * chan), F32),
                pltpu.VMEM((outer, 2 * chan), F32),
                pltpu.VMEM((rows * cols, 2 * chan), F32),
                pltpu.SemaphoreType.DMA((17,)),
                pltpu.SemaphoreType.DMA((17,)),
                pltpu.SemaphoreType.DMA((40,)),
                pltpu.SemaphoreType.DMA((40,)),
                pltpu.SemaphoreType.DMA((4,)),
                pltpu.SemaphoreType.REGULAR((8,)),
            ],
            compiler_params=pltpu.CompilerParams(
                collective_id=0, has_side_effects=True, vmem_limit_bytes=32 * 2**20),
            cost_estimate=pl.CostEstimate(
                flops=4 * frames * rows * cols * 27 * chan * chan, bytes_accessed=3 * 2**20, transcendentals=2**17),
            name="conv_block",
        )(*(pltpu.with_memory_space_constraint(x, pltpu.HBM) for x in (features, conv_first, conv_second)))

    placed = P("tm", "lat", "lon", None)
    return jax.shard_map(local, mesh=mesh, in_specs=(placed, P(), P()), out_specs=placed, check_vma=False)
```

```python
import jax
import jax.numpy as jnp
from jax import lax
from jax.experimental import pallas as pl
from jax.experimental.pallas import tpu as pltpu
from jax.sharding import PartitionSpec as P

MESH = pl.DeviceIdType.MESH
BF16, F32, I32 = jnp.bfloat16, jnp.float32, jnp.int32
F0P, F1P, F0, F1, H0P, H1P, H0, H1 = range(8)
NEXT = {F0: F0P, F1: F1P, H0: H0P, H1: H1P}
E, W, U, UE, UW, D, DE, DW = range(8)
STEP = {E: (1, 0), W: (-1, 0), U: (0, -1), UE: (1, -1), UW: (-1, -1), D: (0, 1), DE: (1, 1), DW: (-1, 1)}
BACK = {E: W, W: E, U: D, D: U, UE: DW, DW: UE, UW: DE, DE: UW}
RIM = {E: 0, W: 1, DE: 2, DW: 3, UE: 4, UW: 5}
T = 16


def block(groups, tiles_lon, tiles_lat, f_ref, k1_ref, k2_ref, o_ref, xc, xl, xr, pack, rim, halo, w1, w2,
          acc_in, acc_out, acc, zsend, zrecv, lsend, lrecv, load, entered):
    tm, lon, lat = lax.axis_index("tm"), lax.axis_index("lon"), lax.axis_index("lat")
    rows, cols, chan = f_ref.shape[1:]
    has_prev, has_next, has_up, has_down = tm > 0, tm < groups - 1, lat > 0, lat < tiles_lat - 1

    ring = tiles_lon // 2

    def lateness(at):
        y = lax.rem(at, ring)
        return jnp.minimum(y, ring - y)

    east, west = lax.rem(lon + 1, tiles_lon), lax.rem(lon + tiles_lon - 1, tiles_lon)
    earlier_e, earlier_w = lateness(east) < lateness(lon), lateness(west) < lateness(lon)
    later_e, later_w = jnp.logical_not(earlier_e), jnp.logical_not(earlier_w)
    far_e, far_w = lax.rem(lon, ring) == ring - 1, lax.rem(lon, ring) == 0
    near_e, near_w = jnp.logical_not(far_e), jnp.logical_not(far_w)
    up, down = lax.rem(lat + tiles_lat - 1, tiles_lat), lax.rem(lat + 1, tiles_lat)

    def device(d):
        step_lon, step_lat = STEP[d]
        to = {}
        if step_lon:
            to["lon"] = east if step_lon > 0 else west
        if step_lat:
            to["lat"] = down if step_lat > 0 else up
        return to

    def toward(ds, *runs):
        def some(rise):
            return [d for d in ds if STEP[d][1] == rise]

        def all_of(ds):
            for run in runs:
                for d in ds:
                    run(d)

        all_of(some(0))
        for rise, cond in ((-1, has_up), (1, has_down)):
            if some(rise):
                pl.when(cond)(lambda rise=rise: all_of(some(rise)))

    barrier = pltpu.get_barrier_semaphore()

    def greet(d):
        pl.semaphore_signal(barrier, inc=1, device_id=device(d), device_id_type=MESH)

    @pl.when(has_prev)
    def _():
        pl.semaphore_signal(barrier, inc=1, device_id={"tm": tm - 1}, device_id_type=MESH)

    origin = jnp.logical_and(tm == 0, jnp.logical_and(lon == 0, lat == 0))
    awake = jnp.logical_not(origin)
    lon_of, lat_of = {0: lon, 1: east, -1: west}, {0: lat, 1: down, -1: up}

    def to_origin(d):
        x, y = STEP[d]
        return jnp.logical_and(tm == 0, jnp.logical_and(lon_of[x] == 0, lat_of[y] == 0))

    def either(a, b):
        return True if a is True or b is True else jnp.logical_or(a, b)

    def greets_me(d):
        first = {U: True, D: True, E: either(near_e, earlier_e), W: near_w}.get(d, earlier_e if STEP[d][0] > 0 else earlier_w)
        if d in (D, DE, DW):
            return either(origin, first)
        return jnp.logical_and(either(origin, first), jnp.logical_not(to_origin(d)))

    def i_greet(d):
        first = {U: True, D: True, E: near_e, W: True}.get(d, later_e if STEP[d][0] > 0 else later_w)
        if d in (D, DE, DW):
            return jnp.logical_and(awake, first)
        return jnp.logical_and(awake, either(first, to_origin(d)))

    def toward_if(cond, ds, *runs):
        toward(ds, *[lambda d, run=run: pl.when(cond(d))(lambda: run(d)) for run in runs])

    toward_if(i_greet, range(8), greet)

    opposite, across, relay = (lax.rem(lon + k, tiles_lon) for k in (ring, ring + 1, ring - 1))

    def relays(d):
        return jnp.logical_not(jnp.logical_and(tm == 0, jnp.logical_and(across == 0, lat_of[STEP[d][1]] == 0)))

    @pl.when(far_e)
    def _():
        pl.semaphore_signal(barrier, inc=1, device_id={"lon": opposite}, device_id_type=MESH)

    @pl.when(jnp.logical_and(far_w, awake))
    def _():
        toward((W, UW, DW), lambda d: pl.semaphore_signal(
            barrier, inc=1, device_id={**device(d), "lon": relay}, device_id_type=MESH))

    EAST, WEST = (E, UE, DE), (W, UW, DW)
    from_last, to_first = jnp.logical_and(lon == 0, has_prev), jnp.logical_and(lon == tiles_lon - 1, has_next)

    @pl.when(from_last)
    def _():
        toward(WEST, lambda d: pl.semaphore_signal(
            barrier, inc=1, device_id={"tm": tm - 1, **device(d)}, device_id_type=MESH))


    over = tiles_lat // 2
    from_over, to_over = jnp.logical_and(lat == over - 1, has_prev), jnp.logical_and(lat == over, has_next)

    @pl.when(from_over)
    def _():
        pl.semaphore_signal(barrier, inc=1, device_id={"tm": tm - 1, "lat": down}, device_id_type=MESH)

    loads = [
        pltpu.make_async_copy(f_ref.at[1], xc.at[F1, pl.ds(1, rows)], load.at[0]),
        pltpu.make_async_copy(f_ref.at[0], xc.at[F0, pl.ds(1, rows)], load.at[1]),
        pltpu.make_async_copy(k1_ref, w1, load.at[2]),
        pltpu.make_async_copy(k2_ref, w2, load.at[3]),
    ]
    for copy in loads:
        copy.start()

    def remote(src, dst, sems, i, to):
        return pltpu.make_async_remote_copy(
            src_ref=src, dst_ref=dst, send_sem=sems[0].at[i], recv_sem=sems[1].at[i], device_id=to, device_id_type=MESH)

    both, past = pl.ds(F0, 2), pl.ds(F0P, 2)
    left, inner, right = pl.ds(0, T), pl.ds(T, cols - 2 * T), pl.ds(cols - T, T)

    PACKS, F1_TOP, F1_LOW, F1_MID, F0_TOP, F0_LOW, F0_MID = range(7)
    H1_HALO, H1_IN, H1_TOP, H1_LOW, H1_LEFT, H1_RIGHT, H0_HALO, H0_TOP, H0_LOW, H0_MID = range(7, 17)

    def forward(i):
        def at(s, *where):
            return xc.at[(s, *where)], xc.at[(NEXT[s], *where)]

        mid = pl.ds(2, rows - 2)
        src, dst = {
            PACKS: lambda: (pack.at[both], pack.at[past]),
            F1_TOP: lambda: at(F1, 1), F1_LOW: lambda: at(F1, rows), F1_MID: lambda: at(F1, mid),
            F0_TOP: lambda: at(F0, 1), F0_LOW: lambda: at(F0, rows), F0_MID: lambda: at(F0, mid),
            H1_HALO: lambda: (halo.at[H1 - 4, 0], halo.at[H1P - 4, 0]),
            H1_IN: lambda: at(H1, mid, inner), H1_TOP: lambda: at(H1, 1), H1_LOW: lambda: at(H1, rows),
            H1_LEFT: lambda: at(H1, mid, left), H1_RIGHT: lambda: at(H1, mid, right),
            H0_HALO: lambda: (halo.at[H0 - 4, 0], halo.at[H0P - 4, 0]),
            H0_TOP: lambda: at(H0, 1), H0_LOW: lambda: at(H0, rows), H0_MID: lambda: at(H0, mid),
        }[i]()
        return remote(src, dst, (zsend, zrecv), i, {"tm": lax.rem(tm + 1, groups)})

    def send_on(*parts):
        pl.when(has_next)(lambda: [forward(p).start() for p in parts] and None)

    def arrived(*parts):
        pl.when(has_prev)(lambda: [forward(p).wait_recv() for p in parts] and None)

    def own(d):
        if d in RIM:
            src, dst = pack.at[both, int(STEP[d][0] > 0)], rim.at[both, RIM[d]]
        else:
            src, dst = xc.at[both, 1 if d == U else rows], xc.at[both, rows + 1 if d == U else 0]
        return remote(src, dst, (lsend, lrecv), d, device(d))

    def past_pack(d):
        return remote(pack.at[past, int(STEP[d][0] > 0)], rim.at[past, RIM[d]], (lsend, lrecv), 8 + d, device(d))

    def direct_pack(d):
        return remote(
            pack.at[both, 1], rim.at[past, RIM[d]], (lsend, lrecv), 8 + d, {"tm": lax.rem(tm + 1, groups), **device(d)})

    def row(s):
        base = {F1P: 8, F0P: 16}.get(s, 24 + 4 * (s - 4))

        def make(d):
            return remote(
                xc.at[s, 1 if d == U else rows], xc.at[s, rows + 1 if d == U else 0],
                (lsend, lrecv), base + (d if s < H0P else int(d == D)), device(d))
        return make

    def halo_of(s):
        def make(d):
            return remote(
                halo.at[s - 4, 0], halo.at[s - 4, 2 if d == U else 1],
                (lsend, lrecv), 26 + 4 * (s - 4) + int(d == D), device(d))
        return make

    def straight(s):
        to, base = {"tm": lax.rem(tm + 1, groups), "lat": up}, {F1: 10, F0: 18}.get(s, 24 + 4 * (NEXT[s] - 4))
        copies = [remote(xc.at[s, 1], xc.at[NEXT[s], rows + 1], (lsend, lrecv), base, to)]
        if s > H1P:
            copies.append(remote(halo.at[s - 4, 0], halo.at[NEXT[s] - 4, 2], (lsend, lrecv), base + 2, to))
        return copies

    def go_straight(s):
        pl.when(to_over)(lambda: [copy.start() for copy in straight(s)] and None)

    def gone_straight(*ss):
        pl.when(to_over)(lambda: [copy.wait_send() for s in ss for copy in straight(s)] and None)

    def pass_on(*runs):
        toward((D,), *runs)
        pl.when(lat != over)(lambda: toward((U,), *runs))

    def send(*makes):
        return [lambda d, make=make: make(d).start() for make in makes]

    def receive(*makes):
        return [lambda d, make=make: make(BACK[d]).wait_recv() for make in makes]

    def sent(*makes):
        return [lambda d, make=make: make(d).wait_send() for make in makes]

    def if_past(run):
        pl.when(has_prev)(run)

    ROWS, SIDES = (U, D), (E, UE, DE, W, UW, DW)

    @pl.when(jnp.logical_not(has_prev))
    def _():
        for s in (F0P, F1P, H0P, H1P):
            xc[s] = jnp.zeros(xc.shape[1:], BF16)
        pack[past] = jnp.zeros((2, *pack.shape[1:]), BF16)
        rim[past] = jnp.zeros((2, *rim.shape[1:]), BF16)
        halo[0:2] = jnp.zeros((2, *halo.shape[1:]), BF16)

    @pl.when(jnp.logical_not(has_up))
    def _():
        for s in range(8):
            xc[s, 0] = jnp.zeros((cols, chan), BF16)
        for s in range(4):
            rim[s, 2:4] = jnp.zeros((2, 2 * rows, chan), BF16)
            halo[s, 1] = jnp.zeros((2 * rows, chan), BF16)

    @pl.when(jnp.logical_not(has_down))
    def _():
        for s in range(8):
            xc[s, rows + 1] = jnp.zeros((cols, chan), BF16)
        for s in range(4):
            rim[s, 4:6] = jnp.zeros((2, 2 * rows, chan), BF16)
            halo[s, 2] = jnp.zeros((2 * rows, chan), BF16)

    def make_pack(s):
        for half, at in ((0, 0), (1, cols - T)):
            tile = [xc[s, r, at:at + T] for r in range(1, rows + 1)]
            js = (0, 1) if half == 0 else (T - 2, T - 1)
            pack[s, half] = jnp.concatenate([x[j:j + 1] for j in js for x in tile], axis=0)

    def beside(s, r):
        if s < H0P:
            if r == 0:
                return rim[s, 2, 2 * rows - 1:], rim[s, 3, rows - 1:rows]
            if r == rows + 1:
                return rim[s, 4, rows:rows + 1], rim[s, 5, 0:1]
            return rim[s, 0, rows + r - 1:rows + r], rim[s, 1, r - 1:r]
        if r == 0:
            return halo[s - 4, 1, rows - 1:rows], halo[s - 4, 1, 2 * rows - 1:]
        if r == rows + 1:
            return halo[s - 4, 2, 0:1], halo[s - 4, 2, rows:rows + 1]
        return halo[s - 4, 0, r - 1:r], halo[s - 4, 0, rows + r - 1:rows + r]

    def shift_in(s):
        for r in range(1, rows + 1):
            x = xc[s, r]
            xl[s, r, T:cols - T] = x[T - 1:cols - T - 1]
            xr[s, r, T:cols - T] = x[T + 1:cols - T + 1]

    def shift_out(s):
        for r in range(rows + 2):
            before, after = beside(s, r)
            x = xc[s, r]
            if r in (0, rows + 1):
                xl[s, r, T:cols - T] = x[T - 1:cols - T - 1]
                xr[s, r, T:cols - T] = x[T + 1:cols - T + 1]
            xl[s, r, 0:T] = jnp.concatenate([before, x[:T - 1]], axis=0)
            xl[s, r, cols - T:] = x[cols - T - 1:cols - 1]
            xr[s, r, 0:T] = x[1:T + 1]
            xr[s, r, cols - T:] = jnp.concatenate([x[cols - T + 1:], after], axis=0)

    def shift_all(s):
        for r in range(rows + 2):
            before, after = beside(s, r)
            x = xc[s, r]
            xl[s, r] = jnp.concatenate([before, x[:cols - 1]], axis=0)
            xr[s, r] = jnp.concatenate([x[1:], after], axis=0)

    def halo_taps(s):
        def column(above, mid, below):
            above, mid, below = above.astype(F32), mid.astype(F32), below.astype(F32)
            return (jnp.concatenate([above, mid[:rows - 1]], axis=0), mid, jnp.concatenate([mid[1:], below], axis=0))

        def rim_column(at, side):
            k = side
            return column(rim[s, k + 2, at + rows - 1:at + rows], rim[s, k, at:at + rows], rim[s, k + 4, at:at + 1])

        first = column(xc[s, 0, 0:1], pack[s, 0, 0:rows], xc[s, rows + 1, 0:1])
        last = column(xc[s, 0, cols - 1:], pack[s, 1, rows:], xc[s, rows + 1, cols - 1:])
        wests = (rim_column(0, 0), rim_column(rows, 0), first)
        easts = (last, rim_column(0, 1), rim_column(rows, 1))
        return jnp.concatenate(
            [jnp.concatenate([wests[c][b], easts[c][b]], axis=0).astype(BF16) for b in range(3) for c in range(3)], axis=1)

    MID, INNER = slice(1, rows - 1), slice(T, cols - T)
    IN = ((MID, INNER),)
    OUT = ((slice(0, rows), slice(0, T)), (slice(0, rows), slice(cols - T, cols)), (slice(0, 1), INNER), (slice(rows - 1, rows), INNER))
    ALL = ((slice(0, rows), slice(0, cols)),)

    def taken(ref, s, b, cuts):
        some = [ref[s, r.start + b:r.stop + b, c].reshape(-1, chan) for r, c in cuts]
        return some[0] if len(some) == 1 else jnp.concatenate(some, axis=0)

    def taps(s, w, times, cuts):
        x = jnp.concatenate([taken(ref, s, b, cuts) for b in range(3) for ref in (xl, xc, xr)], axis=1)
        if cuts is OUT:
            x = jnp.concatenate([x, halo_taps(s)], axis=0)
        k = jnp.concatenate([w[a].reshape(9 * chan, chan) for a in times], axis=1)
        return jnp.dot(x, k, preferred_element_type=F32)

    def shift(s, cuts):
        (shift_in if cuts is IN else shift_out if cuts is OUT else shift_all)(s)

    def own_later(s, w, acc, cuts):
        shift(s, cuts)
        acc[:, chan:] = taps(s, w, (2,), cuts)

    def own_earlier(s, w, acc, cuts):
        shift(s, cuts)
        v = taps(s, w, (2, 1), cuts)
        acc[:, :chan] = v[:, :chan]
        acc[:, chan:] += v[:, chan:]

    def past_later(s, w, acc, cuts):
        shift(s, cuts)
        v = acc[...] + taps(s, w, (1, 0), cuts)
        acc[:, :chan] = v[:, :chan]
        return v[:, chan:]

    def past_earlier(s, w, acc, cuts):
        shift(s, cuts)
        return acc[:, :chan] + taps(s, w, (0,), cuts)

    def silu(v):
        return (v / (1 + jnp.exp(-v))).astype(BF16)

    def hidden_part(s, h, cuts):
        at = 0
        for r, c in cuts:
            high, wide = r.stop - r.start, c.stop - c.start
            xc[s, r.start + 1:r.stop + 1, c] = h[at:at + high * wide].reshape(high, wide, chan)
            at += high * wide
        return at

    def hidden_in(s, v):
        hidden_part(s, silu(v), IN)

    def hidden_out(s, v):
        h = silu(v)
        at = hidden_part(s, h, OUT)
        halo[s - 4, 0] = h[at:]

    def result(t, v):
        x = xc[(F0, F1)[t], 1:rows + 1].reshape(-1, chan).astype(F32) + v
        o_ref[t] = x.astype(BF16).reshape(rows, cols, chan)

    for s, copy in ((F1, loads[0]), (F0, loads[1])):
        copy.wait()
        make_pack(s)

    def count(d):
        there = (has_up, True, has_down)[STEP[d][1] + 1]
        return (greets_me(d) if there is True else jnp.logical_and(there, greets_me(d))).astype(I32)

    pl.semaphore_wait(
        barrier, has_next.astype(I32) + sum(count(d) for d in range(8))
        + far_e.astype(I32) * (1 + relays(E).astype(I32) + jnp.logical_and(has_up, relays(UE)).astype(I32)
                               + jnp.logical_and(has_down, relays(DE)).astype(I32))
        + to_over.astype(I32) + to_first.astype(I32) * (1 + has_up.astype(I32) + has_down.astype(I32)))

    send_on(PACKS)
    pl.when(to_first)(lambda: toward(EAST, *send(direct_pack)))
    send_on(F1_TOP, F1_LOW)
    go_straight(F1)
    send_on(F1_MID, F0_TOP, F0_LOW)
    go_straight(F0)
    send_on(F0_MID)

    def tell(d):
        to = device(d)
        if d in EAST:
            to["lon"] = jnp.where(far_e, across, east)
        pl.semaphore_signal(entered.at[BACK[d]], inc=1, device_id=to, device_id_type=MESH)

    def i_tell(d):
        quiet = jnp.logical_not(i_greet(d))
        return jnp.where(far_e, relays(d), quiet) if d in EAST else quiet

    def told(d):
        pl.semaphore_wait(entered.at[d], 1)

    toward_if(i_tell, range(8), tell)

    def known(ds, *runs):
        toward(ds, lambda d: pl.when(greets_me(d))(lambda: [run(d) for run in runs] and None))

    def late(d):
        return False if d in (D, DE, DW) else to_origin(d)

    def soon(d):
        return jnp.logical_not(jnp.logical_or(greets_me(d), late(d)))

    def last(d):
        return jnp.logical_and(jnp.logical_not(greets_me(d)), late(d))

    def send_past_pack(d):
        if d in EAST:
            pl.when(jnp.logical_and(has_prev, inland))(lambda: past_pack(d).start())
        else:
            if_past(lambda: past_pack(d).start())

    def after_word(cond):
        def run(d):
            told(d)
            own(d).start()
            if d in RIM:
                send_past_pack(d)
        toward(ROWS + SIDES, lambda d: pl.when(cond(d))(lambda: run(d)))

    known(ROWS + SIDES, *send(own))
    loads[2].wait()
    own_later(F1, w1, acc_in, IN)
    own_earlier(F0, w1, acc_in, IN)
    arrived(PACKS)
    if_past(lambda: known(WEST, *send(past_pack)))
    inland = lon < tiles_lon - 1
    pl.when(jnp.logical_and(has_prev, inland))(lambda: known(EAST, *send(past_pack)))
    arrived(F1_TOP, F1_LOW)
    if_past(lambda: pass_on(*send(row(F1P))))
    after_word(soon)
    arrived(F1_MID)
    hidden_in(H1, past_later(F1P, w1, acc_in, IN))
    send_on(H1_IN)
    arrived(F0_TOP, F0_LOW)
    if_past(lambda: pass_on(*send(row(F0P))))
    after_word(last)

    toward(ROWS + SIDES, *receive(own))
    own_later(F1, w1, acc_out, OUT)
    own_earlier(F0, w1, acc_out, OUT)

    def inner_earlier():
        arrived(F0_MID)
        hidden_in(H0, past_earlier(F0P, w1, acc_in, IN))

    far = jnp.logical_or(far_e, far_w)
    pl.when(far)(inner_earlier)
    if_past(lambda: toward(SIDES, *receive(past_pack)))
    if_past(lambda: toward(ROWS, *receive(row(F1P))))
    hidden_out(H1, past_later(F1P, w1, acc_out, OUT))
    send_on(H1_HALO, H1_TOP, H1_LOW)
    go_straight(H1)
    send_on(H1_LEFT, H1_RIGHT)
    toward(ROWS, *send(row(H1), halo_of(H1)))
    pl.when(jnp.logical_not(far))(inner_earlier)
    if_past(lambda: toward(ROWS, *receive(row(F0P))))
    hidden_out(H0, past_earlier(F0P, w1, acc_out, OUT))
    send_on(H0_HALO, H0_TOP, H0_LOW)
    go_straight(H0)
    send_on(H0_MID)
    toward(ROWS, *send(row(H0), halo_of(H0)))

    loads[3].wait()
    pl.when(has_next)(lambda: [forward(p).wait_send() for p in range(H1_HALO)] and None)
    toward(ROWS + SIDES, *sent(own))
    pl.when(to_first)(lambda: toward(EAST, *sent(direct_pack)))
    gone_straight(F1, F0)

    @pl.when(has_prev)
    def _():
        toward(WEST, *sent(past_pack))
        pl.when(inland)(lambda: toward(EAST, *sent(past_pack)))
        pass_on(*sent(row(F1P), row(F0P)))

    arrived(H1_HALO, H1_TOP, H1_LOW)
    if_past(lambda: pass_on(*send(row(H1P), halo_of(H1P))))
    toward(ROWS, *receive(row(H1), halo_of(H1)))
    own_later(H1, w2, acc, ALL)
    arrived(H0_HALO, H0_TOP, H0_LOW)
    if_past(lambda: pass_on(*send(row(H0P), halo_of(H0P))))
    toward(ROWS, *receive(row(H0), halo_of(H0)))
    own_earlier(H0, w2, acc, ALL)
    pl.when(has_next)(lambda: [forward(p).wait_send() for p in range(H1_HALO, 17)] and None)
    gone_straight(H1, H0)
    toward(ROWS, *sent(row(H0), halo_of(H0), row(H1), halo_of(H1)))
    if_past(lambda: toward(ROWS, *receive(row(H1P), halo_of(H1P))))
    arrived(H1_IN, H1_LEFT, H1_RIGHT)
    result(1, past_later(H1P, w2, acc, ALL))
    arrived(H0_MID)
    if_past(lambda: toward(ROWS, *receive(row(H0P), halo_of(H0P))))
    result(0, past_earlier(H0P, w2, acc, ALL))
    if_past(lambda: pass_on(*sent(row(H1P), halo_of(H1P), row(H0P), halo_of(H0P))))


def solution(mesh):
    groups, tiles_lon, tiles_lat = mesh.shape["tm"], mesh.shape["lon"], mesh.shape["lat"]

    def local(features, conv_first, conv_second):
        frames, rows, cols, chan = features.shape
        frame = (8, rows + 2, cols, chan)
        inner = (cols - 2 * T) * (rows - 2)
        outer = rows * cols - inner + 2 * rows

        def kernel(*refs):
            block(groups, tiles_lon, tiles_lat, *refs)

        return pl.pallas_call(
            kernel,
            out_shape=pltpu.VMEM(features.shape, BF16),
            in_specs=[pl.BlockSpec(memory_space=pltpu.HBM)] * 3,
            out_specs=pl.BlockSpec(memory_space=pltpu.VMEM),
            scratch_shapes=[
                pltpu.VMEM(frame, BF16),
                pltpu.VMEM(frame, BF16),
                pltpu.VMEM(frame, BF16),
                pltpu.VMEM((4, 2, 2 * rows, chan), BF16),
                pltpu.VMEM((4, 6, 2 * rows, chan), BF16),
                pltpu.VMEM((4, 3, 2 * rows, chan), BF16),
                pltpu.VMEM(conv_first.shape, BF16),
                pltpu.VMEM(conv_second.shape, BF16),
                pltpu.VMEM((inner, 2 * chan), F32),
                pltpu.VMEM((outer, 2 * chan), F32),
                pltpu.VMEM((rows * cols, 2 * chan), F32),
                pltpu.SemaphoreType.DMA((17,)),
                pltpu.SemaphoreType.DMA((17,)),
                pltpu.SemaphoreType.DMA((40,)),
                pltpu.SemaphoreType.DMA((40,)),
                pltpu.SemaphoreType.DMA((4,)),
                pltpu.SemaphoreType.REGULAR((8,)),
            ],
            compiler_params=pltpu.CompilerParams(
                collective_id=0, has_side_effects=True, vmem_limit_bytes=32 * 2**20),
            cost_estimate=pl.CostEstimate(
                flops=4 * frames * rows * cols * 27 * chan * chan, bytes_accessed=3 * 2**20, transcendentals=2**17),
            name="conv_block",
        )(*(pltpu.with_memory_space_constraint(x, pltpu.HBM) for x in (features, conv_first, conv_second)))

    placed = P("tm", "lat", "lon", None)
    return jax.shard_map(local, mesh=mesh, in_specs=(placed, P(), P()), out_specs=placed, check_vma=False)
```

```python
import jax
import jax.numpy as jnp
from jax import lax
from jax.experimental import pallas as pl
from jax.experimental.pallas import tpu as pltpu
from jax.sharding import PartitionSpec as P

MESH = pl.DeviceIdType.MESH
BF16, F32, I32 = jnp.bfloat16, jnp.float32, jnp.int32
F0P, F1P, F0, F1, H0P, H1P, H0, H1 = range(8)
NEXT = {F0: F0P, F1: F1P, H0: H0P, H1: H1P}
E, W, U, UE, UW, D, DE, DW = range(8)
STEP = {E: (1, 0), W: (-1, 0), U: (0, -1), UE: (1, -1), UW: (-1, -1), D: (0, 1), DE: (1, 1), DW: (-1, 1)}
BACK = {E: W, W: E, U: D, D: U, UE: DW, DW: UE, UW: DE, DE: UW}
RIM = {E: 0, W: 1, DE: 2, DW: 3, UE: 4, UW: 5}
T = 16


def block(groups, tiles_lon, tiles_lat, f_ref, k1_ref, k2_ref, o_ref, xc, xl, xr, pack, rim, halo, w1, w2,
          acc_in, acc_out, acc, zsend, zrecv, lsend, lrecv, load, entered):
    tm, lon, lat = lax.axis_index("tm"), lax.axis_index("lon"), lax.axis_index("lat")
    rows, cols, chan = f_ref.shape[1:]
    has_prev, has_next, has_up, has_down = tm > 0, tm < groups - 1, lat > 0, lat < tiles_lat - 1

    ring = tiles_lon // 2

    def lateness(at):
        y = lax.rem(at, ring)
        return jnp.minimum(y, ring - y)

    east, west = lax.rem(lon + 1, tiles_lon), lax.rem(lon + tiles_lon - 1, tiles_lon)
    earlier_e, earlier_w = lateness(east) < lateness(lon), lateness(west) < lateness(lon)
    later_e, later_w = jnp.logical_not(earlier_e), jnp.logical_not(earlier_w)
    far_e, far_w = lax.rem(lon, ring) == ring - 1, lax.rem(lon, ring) == 0
    near_e, near_w = jnp.logical_not(far_e), jnp.logical_not(far_w)
    up, down = lax.rem(lat + tiles_lat - 1, tiles_lat), lax.rem(lat + 1, tiles_lat)

    def device(d):
        step_lon, step_lat = STEP[d]
        to = {}
        if step_lon:
            to["lon"] = east if step_lon > 0 else west
        if step_lat:
            to["lat"] = down if step_lat > 0 else up
        return to

    def toward(ds, *runs):
        def some(rise):
            return [d for d in ds if STEP[d][1] == rise]

        def all_of(ds):
            for run in runs:
                for d in ds:
                    run(d)

        all_of(some(0))
        for rise, cond in ((-1, has_up), (1, has_down)):
            if some(rise):
                pl.when(cond)(lambda rise=rise: all_of(some(rise)))

    barrier = pltpu.get_barrier_semaphore()

    def greet(d):
        pl.semaphore_signal(barrier, inc=1, device_id=device(d), device_id_type=MESH)

    @pl.when(has_prev)
    def _():
        pl.semaphore_signal(barrier, inc=1, device_id={"tm": tm - 1}, device_id_type=MESH)

    origin = jnp.logical_and(tm == 0, jnp.logical_and(lon == 0, lat == 0))
    awake = jnp.logical_not(origin)
    lon_of, lat_of = {0: lon, 1: east, -1: west}, {0: lat, 1: down, -1: up}

    def to_origin(d):
        x, y = STEP[d]
        return jnp.logical_and(tm == 0, jnp.logical_and(lon_of[x] == 0, lat_of[y] == 0))

    def either(a, b):
        return True if a is True or b is True else jnp.logical_or(a, b)

    def greets_me(d):
        first = {U: True, D: True, E: either(near_e, earlier_e), W: near_w}.get(d, earlier_e if STEP[d][0] > 0 else earlier_w)
        if d in (D, DE, DW):
            return either(origin, first)
        return jnp.logical_and(either(origin, first), jnp.logical_not(to_origin(d)))

    def i_greet(d):
        first = {U: True, D: True, E: near_e, W: True}.get(d, later_e if STEP[d][0] > 0 else later_w)
        if d in (D, DE, DW):
            return jnp.logical_and(awake, first)
        return jnp.logical_and(awake, either(first, to_origin(d)))

    def toward_if(cond, ds, *runs):
        toward(ds, *[lambda d, run=run: pl.when(cond(d))(lambda: run(d)) for run in runs])

    toward_if(i_greet, range(8), greet)

    opposite, across, relay = (lax.rem(lon + k, tiles_lon) for k in (ring, ring + 1, ring - 1))

    def relays(d):
        return jnp.logical_not(jnp.logical_and(tm == 0, jnp.logical_and(across == 0, lat_of[STEP[d][1]] == 0)))

    @pl.when(far_e)
    def _():
        pl.semaphore_signal(barrier, inc=1, device_id={"lon": opposite}, device_id_type=MESH)

    @pl.when(jnp.logical_and(far_w, awake))
    def _():
        toward((W, UW, DW), lambda d: pl.semaphore_signal(
            barrier, inc=1, device_id={**device(d), "lon": relay}, device_id_type=MESH))

    EAST, WEST = (E, UE, DE), (W, UW, DW)
    from_last, to_first = jnp.logical_and(lon == 0, has_prev), jnp.logical_and(lon == tiles_lon - 1, has_next)

    @pl.when(from_last)
    def _():
        toward(WEST, lambda d: pl.semaphore_signal(
            barrier, inc=1, device_id={"tm": tm - 1, **device(d)}, device_id_type=MESH))


    over = tiles_lat // 2
    from_over, to_over = jnp.logical_and(lat == over - 1, has_prev), jnp.logical_and(lat == over, has_next)

    @pl.when(from_over)
    def _():
        pl.semaphore_signal(barrier, inc=1, device_id={"tm": tm - 1, "lat": down}, device_id_type=MESH)

    loads = [
        pltpu.make_async_copy(f_ref.at[1], xc.at[F1, pl.ds(1, rows)], load.at[0]),
        pltpu.make_async_copy(f_ref.at[0], xc.at[F0, pl.ds(1, rows)], load.at[1]),
        pltpu.make_async_copy(k1_ref, w1, load.at[2]),
        pltpu.make_async_copy(k2_ref, w2, load.at[3]),
    ]
    for copy in loads:
        copy.start()

    def remote(src, dst, sems, i, to):
        return pltpu.make_async_remote_copy(
            src_ref=src, dst_ref=dst, send_sem=sems[0].at[i], recv_sem=sems[1].at[i], device_id=to, device_id_type=MESH)

    both, past = pl.ds(F0, 2), pl.ds(F0P, 2)
    left, inner, right = pl.ds(0, T), pl.ds(T, cols - 2 * T), pl.ds(cols - T, T)

    PACKS, F1_TOP, F1_LOW, F1_MID, F0_TOP, F0_LOW, F0_MID = range(7)
    H1_HALO, H1_IN, H1_TOP, H1_LOW, H1_LEFT, H1_RIGHT, H0_HALO, H0_TOP, H0_LOW, H0_MID = range(7, 17)

    def forward(i):
        def at(s, *where):
            return xc.at[(s, *where)], xc.at[(NEXT[s], *where)]

        mid = pl.ds(2, rows - 2)
        src, dst = {
            PACKS: lambda: (pack.at[both], pack.at[past]),
            F1_TOP: lambda: at(F1, 1), F1_LOW: lambda: at(F1, rows), F1_MID: lambda: at(F1, mid),
            F0_TOP: lambda: at(F0, 1), F0_LOW: lambda: at(F0, rows), F0_MID: lambda: at(F0, mid),
            H1_HALO: lambda: (halo.at[H1 - 4, 0], halo.at[H1P - 4, 0]),
            H1_IN: lambda: at(H1, mid, inner), H1_TOP: lambda: at(H1, 1), H1_LOW: lambda: at(H1, rows),
            H1_LEFT: lambda: at(H1, mid, left), H1_RIGHT: lambda: at(H1, mid, right),
            H0_HALO: lambda: (halo.at[H0 - 4, 0], halo.at[H0P - 4, 0]),
            H0_TOP: lambda: at(H0, 1), H0_LOW: lambda: at(H0, rows), H0_MID: lambda: at(H0, mid),
        }[i]()
        return remote(src, dst, (zsend, zrecv), i, {"tm": lax.rem(tm + 1, groups)})

    def send_on(*parts):
        pl.when(has_next)(lambda: [forward(p).start() for p in parts] and None)

    def arrived(*parts):
        pl.when(has_prev)(lambda: [forward(p).wait_recv() for p in parts] and None)

    def own(d):
        if d in RIM:
            src, dst = pack.at[both, int(STEP[d][0] > 0)], rim.at[both, RIM[d]]
        else:
            src, dst = xc.at[both, 1 if d == U else rows], xc.at[both, rows + 1 if d == U else 0]
        return remote(src, dst, (lsend, lrecv), d, device(d))

    def past_pack(d):
        return remote(pack.at[past, int(STEP[d][0] > 0)], rim.at[past, RIM[d]], (lsend, lrecv), 8 + d, device(d))

    def direct_pack(d):
        return remote(
            pack.at[both, 1], rim.at[past, RIM[d]], (lsend, lrecv), 8 + d, {"tm": lax.rem(tm + 1, groups), **device(d)})

    def row(s):
        base = {F1P: 8, F0P: 16}.get(s, 24 + 4 * (s - 4))

        def make(d):
            return remote(
                xc.at[s, 1 if d == U else rows], xc.at[s, rows + 1 if d == U else 0],
                (lsend, lrecv), base + (d if s < H0P else int(d == D)), device(d))
        return make

    def halo_of(s):
        def make(d):
            return remote(
                halo.at[s - 4, 0], halo.at[s - 4, 2 if d == U else 1],
                (lsend, lrecv), 26 + 4 * (s - 4) + int(d == D), device(d))
        return make

    def straight(s):
        to, base = {"tm": lax.rem(tm + 1, groups), "lat": up}, {F1: 10, F0: 18}.get(s, 24 + 4 * (NEXT[s] - 4))
        copies = [remote(xc.at[s, 1], xc.at[NEXT[s], rows + 1], (lsend, lrecv), base, to)]
        if s > H1P:
            copies.append(remote(halo.at[s - 4, 0], halo.at[NEXT[s] - 4, 2], (lsend, lrecv), base + 2, to))
        return copies

    def go_straight(s):
        pl.when(to_over)(lambda: [copy.start() for copy in straight(s)] and None)

    def gone_straight(*ss):
        pl.when(to_over)(lambda: [copy.wait_send() for s in ss for copy in straight(s)] and None)

    def pass_on(*runs):
        toward((D,), *runs)
        pl.when(lat != over)(lambda: toward((U,), *runs))

    def send(*makes):
        return [lambda d, make=make: make(d).start() for make in makes]

    def receive(*makes):
        return [lambda d, make=make: make(BACK[d]).wait_recv() for make in makes]

    def sent(*makes):
        return [lambda d, make=make: make(d).wait_send() for make in makes]

    def if_past(run):
        pl.when(has_prev)(run)

    ROWS, SIDES = (U, D), (E, UE, DE, W, UW, DW)

    @pl.when(jnp.logical_not(has_prev))
    def _():
        for s in (F0P, F1P, H0P, H1P):
            xc[s] = jnp.zeros(xc.shape[1:], BF16)
        pack[past] = jnp.zeros((2, *pack.shape[1:]), BF16)
        rim[past] = jnp.zeros((2, *rim.shape[1:]), BF16)
        halo[0:2] = jnp.zeros((2, *halo.shape[1:]), BF16)

    @pl.when(jnp.logical_not(has_up))
    def _():
        for s in range(8):
            xc[s, 0] = jnp.zeros((cols, chan), BF16)
        for s in range(4):
            rim[s, 2:4] = jnp.zeros((2, 2 * rows, chan), BF16)
            halo[s, 1] = jnp.zeros((2 * rows, chan), BF16)

    @pl.when(jnp.logical_not(has_down))
    def _():
        for s in range(8):
            xc[s, rows + 1] = jnp.zeros((cols, chan), BF16)
        for s in range(4):
            rim[s, 4:6] = jnp.zeros((2, 2 * rows, chan), BF16)
            halo[s, 2] = jnp.zeros((2 * rows, chan), BF16)

    def make_pack(s):
        for half, at in ((0, 0), (1, cols - T)):
            tile = [xc[s, r, at:at + T] for r in range(1, rows + 1)]
            js = (0, 1) if half == 0 else (T - 2, T - 1)
            pack[s, half] = jnp.concatenate([x[j:j + 1] for j in js for x in tile], axis=0)

    def beside(s, r):
        if s < H0P:
            if r == 0:
                return rim[s, 2, 2 * rows - 1:], rim[s, 3, rows - 1:rows]
            if r == rows + 1:
                return rim[s, 4, rows:rows + 1], rim[s, 5, 0:1]
            return rim[s, 0, rows + r - 1:rows + r], rim[s, 1, r - 1:r]
        if r == 0:
            return halo[s - 4, 1, rows - 1:rows], halo[s - 4, 1, 2 * rows - 1:]
        if r == rows + 1:
            return halo[s - 4, 2, 0:1], halo[s - 4, 2, rows:rows + 1]
        return halo[s - 4, 0, r - 1:r], halo[s - 4, 0, rows + r - 1:rows + r]

    def shift_in(s):
        for r in range(1, rows + 1):
            x = xc[s, r]
            xl[s, r, T:cols - T] = x[T - 1:cols - T - 1]
            xr[s, r, T:cols - T] = x[T + 1:cols - T + 1]

    def shift_out(s):
        for r in range(rows + 2):
            before, after = beside(s, r)
            x = xc[s, r]
            if r in (0, rows + 1):
                xl[s, r, T:cols - T] = x[T - 1:cols - T - 1]
                xr[s, r, T:cols - T] = x[T + 1:cols - T + 1]
            xl[s, r, 0:T] = jnp.concatenate([before, x[:T - 1]], axis=0)
            xl[s, r, cols - T:] = x[cols - T - 1:cols - 1]
            xr[s, r, 0:T] = x[1:T + 1]
            xr[s, r, cols - T:] = jnp.concatenate([x[cols - T + 1:], after], axis=0)

    def shift_all(s):
        for r in range(rows + 2):
            before, after = beside(s, r)
            x = xc[s, r]
            xl[s, r] = jnp.concatenate([before, x[:cols - 1]], axis=0)
            xr[s, r] = jnp.concatenate([x[1:], after], axis=0)

    def halo_taps(s):
        def column(above, mid, below):
            above, mid, below = above.astype(F32), mid.astype(F32), below.astype(F32)
            return (jnp.concatenate([above, mid[:rows - 1]], axis=0), mid, jnp.concatenate([mid[1:], below], axis=0))

        def rim_column(at, side):
            k = side
            return column(rim[s, k + 2, at + rows - 1:at + rows], rim[s, k, at:at + rows], rim[s, k + 4, at:at + 1])

        first = column(xc[s, 0, 0:1], pack[s, 0, 0:rows], xc[s, rows + 1, 0:1])
        last = column(xc[s, 0, cols - 1:], pack[s, 1, rows:], xc[s, rows + 1, cols - 1:])
        wests = (rim_column(0, 0), rim_column(rows, 0), first)
        easts = (last, rim_column(0, 1), rim_column(rows, 1))
        return jnp.concatenate(
            [jnp.concatenate([wests[c][b], easts[c][b]], axis=0).astype(BF16) for b in range(3) for c in range(3)], axis=1)

    MID, INNER = slice(1, rows - 1), slice(T, cols - T)
    IN = ((MID, INNER),)
    OUT = ((slice(0, rows), slice(0, T)), (slice(0, rows), slice(cols - T, cols)), (slice(0, 1), INNER), (slice(rows - 1, rows), INNER))
    ALL = ((slice(0, rows), slice(0, cols)),)

    def taken(ref, s, b, cuts):
        some = [ref[s, r.start + b:r.stop + b, c].reshape(-1, chan) for r, c in cuts]
        return some[0] if len(some) == 1 else jnp.concatenate(some, axis=0)

    def taps(s, w, times, cuts):
        x = jnp.concatenate([taken(ref, s, b, cuts) for b in range(3) for ref in (xl, xc, xr)], axis=1)
        if cuts is OUT:
            x = jnp.concatenate([x, halo_taps(s)], axis=0)
        k = jnp.concatenate([w[a].reshape(9 * chan, chan) for a in times], axis=1)
        return jnp.dot(x, k, preferred_element_type=F32)

    def shift(s, cuts):
        (shift_in if cuts is IN else shift_out if cuts is OUT else shift_all)(s)

    def own_later(s, w, acc, cuts):
        shift(s, cuts)
        acc[:, chan:] = taps(s, w, (2,), cuts)

    def own_earlier(s, w, acc, cuts):
        shift(s, cuts)
        v = taps(s, w, (2, 1), cuts)
        acc[:, :chan] = v[:, :chan]
        acc[:, chan:] += v[:, chan:]

    def past_later(s, w, acc, cuts):
        shift(s, cuts)
        v = acc[...] + taps(s, w, (1, 0), cuts)
        acc[:, :chan] = v[:, :chan]
        return v[:, chan:]

    def past_earlier(s, w, acc, cuts):
        shift(s, cuts)
        return acc[:, :chan] + taps(s, w, (0,), cuts)

    def silu(v):
        return (v / (1 + jnp.exp(-v))).astype(BF16)

    def hidden_part(s, h, cuts):
        at = 0
        for r, c in cuts:
            high, wide = r.stop - r.start, c.stop - c.start
            xc[s, r.start + 1:r.stop + 1, c] = h[at:at + high * wide].reshape(high, wide, chan)
            at += high * wide
        return at

    def hidden_in(s, v):
        hidden_part(s, silu(v), IN)

    def hidden_out(s, v):
        h = silu(v)
        at = hidden_part(s, h, OUT)
        halo[s - 4, 0] = h[at:]

    def result(t, v):
        x = xc[(F0, F1)[t], 1:rows + 1].reshape(-1, chan).astype(F32) + v
        o_ref[t] = x.astype(BF16).reshape(rows, cols, chan)

    for s, copy in ((F1, loads[0]), (F0, loads[1])):
        copy.wait()
        make_pack(s)

    def count(d):
        there = (has_up, True, has_down)[STEP[d][1] + 1]
        return (greets_me(d) if there is True else jnp.logical_and(there, greets_me(d))).astype(I32)

    pl.semaphore_wait(
        barrier, has_next.astype(I32) + sum(count(d) for d in range(8))
        + far_e.astype(I32) * (1 + relays(E).astype(I32) + jnp.logical_and(has_up, relays(UE)).astype(I32)
                               + jnp.logical_and(has_down, relays(DE)).astype(I32))
        + to_over.astype(I32) + to_first.astype(I32) * (1 + has_up.astype(I32) + has_down.astype(I32)))

    send_on(PACKS)
    pl.when(to_first)(lambda: toward(EAST, *send(direct_pack)))
    send_on(F1_TOP, F1_LOW)
    go_straight(F1)
    send_on(F1_MID, F0_TOP, F0_LOW)
    go_straight(F0)
    send_on(F0_MID)

    def tell(d):
        to = device(d)
        if d in EAST:
            to["lon"] = jnp.where(far_e, across, east)
        pl.semaphore_signal(entered.at[BACK[d]], inc=1, device_id=to, device_id_type=MESH)

    def i_tell(d):
        quiet = jnp.logical_not(i_greet(d))
        if d in EAST:
            return jnp.where(far_e, relays(d), quiet)
        return jnp.logical_and(quiet, awake) if d in WEST else quiet

    helper = jnp.logical_and(tm == 0, jnp.logical_and(lon == 0, lat == 1))

    def direct(d):
        if d not in (E, UE):
            return True
        return jnp.logical_not(jnp.logical_and(to_origin(d), lon == tiles_lon - 1))

    def helped():
        return [
            pltpu.make_async_remote_copy(
                src_ref=rim.at[both, src], dst_ref=rim.at[both, dst], send_sem=lsend.at[40 + i], recv_sem=lrecv.at[d],
                device_id={"lat": up}, device_id_type=MESH)
            for i, (src, dst, d) in enumerate(((RIM[DE], RIM[E], E), (RIM[E], RIM[UE], UE)))]

    def told(d):
        pl.semaphore_wait(entered.at[d], 1)

    toward_if(i_tell, range(8), tell)

    def known(ds, *runs):
        toward(ds, lambda d: pl.when(greets_me(d))(lambda: [run(d) for run in runs] and None))

    def late(d):
        return False if d in (D, DE, DW) else to_origin(d)

    def soon(d):
        return jnp.logical_not(jnp.logical_or(greets_me(d), late(d)))

    def last(d):
        slow = jnp.logical_and(jnp.logical_not(greets_me(d)), late(d))
        return slow if direct(d) is True else jnp.logical_and(slow, direct(d))

    def send_past_pack(d):
        if d in EAST:
            pl.when(jnp.logical_and(has_prev, inland))(lambda: past_pack(d).start())
        else:
            if_past(lambda: past_pack(d).start())

    def after_word(cond):
        def run(d):
            told(d)
            own(d).start()
            if d in RIM:
                send_past_pack(d)
        toward(ROWS + SIDES, lambda d: pl.when(cond(d))(lambda: run(d)))

    known(ROWS + SIDES, *send(own))
    loads[2].wait()
    own_later(F1, w1, acc_in, IN)
    own_earlier(F0, w1, acc_in, IN)
    arrived(PACKS)
    if_past(lambda: known(WEST, *send(past_pack)))
    inland = lon < tiles_lon - 1
    pl.when(jnp.logical_and(has_prev, inland))(lambda: known(EAST, *send(past_pack)))
    arrived(F1_TOP, F1_LOW)
    if_past(lambda: pass_on(*send(row(F1P))))
    after_word(soon)
    arrived(F1_MID)
    hidden_in(H1, past_later(F1P, w1, acc_in, IN))
    send_on(H1_IN)
    arrived(F0_TOP, F0_LOW)
    if_past(lambda: pass_on(*send(row(F0P))))
    after_word(last)

    toward(ROWS + SIDES, *receive(own))
    pl.when(helper)(lambda: [copy.start() for copy in helped()] and None)
    own_later(F1, w1, acc_out, OUT)
    own_earlier(F0, w1, acc_out, OUT)

    def inner_earlier():
        arrived(F0_MID)
        hidden_in(H0, past_earlier(F0P, w1, acc_in, IN))

    far = jnp.logical_or(far_e, far_w)
    pl.when(far)(inner_earlier)
    if_past(lambda: toward(SIDES, *receive(past_pack)))
    if_past(lambda: toward(ROWS, *receive(row(F1P))))
    hidden_out(H1, past_later(F1P, w1, acc_out, OUT))
    send_on(H1_HALO, H1_TOP, H1_LOW)
    go_straight(H1)
    send_on(H1_LEFT, H1_RIGHT)
    toward(ROWS, *send(row(H1), halo_of(H1)))
    pl.when(jnp.logical_not(far))(inner_earlier)
    if_past(lambda: toward(ROWS, *receive(row(F0P))))
    hidden_out(H0, past_earlier(F0P, w1, acc_out, OUT))
    send_on(H0_HALO, H0_TOP, H0_LOW)
    go_straight(H0)
    send_on(H0_MID)
    toward(ROWS, *send(row(H0), halo_of(H0)))

    loads[3].wait()
    pl.when(has_next)(lambda: [forward(p).wait_send() for p in range(H1_HALO)] and None)
    toward((U, D, DE, W, UW, DW), *sent(own))
    toward_if(direct, (E, UE), *sent(own))
    pl.when(helper)(lambda: [copy.wait_send() for copy in helped()] and None)
    pl.when(to_first)(lambda: toward(EAST, *sent(direct_pack)))
    gone_straight(F1, F0)

    @pl.when(has_prev)
    def _():
        toward(WEST, *sent(past_pack))
        pl.when(inland)(lambda: toward(EAST, *sent(past_pack)))
        pass_on(*sent(row(F1P), row(F0P)))

    arrived(H1_HALO, H1_TOP, H1_LOW)
    if_past(lambda: pass_on(*send(row(H1P), halo_of(H1P))))
    toward(ROWS, *receive(row(H1), halo_of(H1)))
    own_later(H1, w2, acc, ALL)
    arrived(H0_HALO, H0_TOP, H0_LOW)
    if_past(lambda: pass_on(*send(row(H0P), halo_of(H0P))))
    toward(ROWS, *receive(row(H0), halo_of(H0)))
    own_earlier(H0, w2, acc, ALL)
    pl.when(has_next)(lambda: [forward(p).wait_send() for p in range(H1_HALO, 17)] and None)
    gone_straight(H1, H0)
    toward(ROWS, *sent(row(H0), halo_of(H0), row(H1), halo_of(H1)))
    if_past(lambda: toward(ROWS, *receive(row(H1P), halo_of(H1P))))
    arrived(H1_IN, H1_LEFT, H1_RIGHT)
    result(1, past_later(H1P, w2, acc, ALL))
    arrived(H0_MID)
    if_past(lambda: toward(ROWS, *receive(row(H0P), halo_of(H0P))))
    result(0, past_earlier(H0P, w2, acc, ALL))
    if_past(lambda: pass_on(*sent(row(H1P), halo_of(H1P), row(H0P), halo_of(H0P))))


def solution(mesh):
    groups, tiles_lon, tiles_lat = mesh.shape["tm"], mesh.shape["lon"], mesh.shape["lat"]

    def local(features, conv_first, conv_second):
        frames, rows, cols, chan = features.shape
        frame = (8, rows + 2, cols, chan)
        inner = (cols - 2 * T) * (rows - 2)
        outer = rows * cols - inner + 2 * rows

        def kernel(*refs):
            block(groups, tiles_lon, tiles_lat, *refs)

        return pl.pallas_call(
            kernel,
            out_shape=pltpu.VMEM(features.shape, BF16),
            in_specs=[pl.BlockSpec(memory_space=pltpu.HBM)] * 3,
            out_specs=pl.BlockSpec(memory_space=pltpu.VMEM),
            scratch_shapes=[
                pltpu.VMEM(frame, BF16),
                pltpu.VMEM(frame, BF16),
                pltpu.VMEM(frame, BF16),
                pltpu.VMEM((4, 2, 2 * rows, chan), BF16),
                pltpu.VMEM((4, 6, 2 * rows, chan), BF16),
                pltpu.VMEM((4, 3, 2 * rows, chan), BF16),
                pltpu.VMEM(conv_first.shape, BF16),
                pltpu.VMEM(conv_second.shape, BF16),
                pltpu.VMEM((inner, 2 * chan), F32),
                pltpu.VMEM((outer, 2 * chan), F32),
                pltpu.VMEM((rows * cols, 2 * chan), F32),
                pltpu.SemaphoreType.DMA((17,)),
                pltpu.SemaphoreType.DMA((17,)),
                pltpu.SemaphoreType.DMA((42,)),
                pltpu.SemaphoreType.DMA((40,)),
                pltpu.SemaphoreType.DMA((4,)),
                pltpu.SemaphoreType.REGULAR((8,)),
            ],
            compiler_params=pltpu.CompilerParams(
                collective_id=0, has_side_effects=True, vmem_limit_bytes=32 * 2**20),
            cost_estimate=pl.CostEstimate(
                flops=4 * frames * rows * cols * 27 * chan * chan, bytes_accessed=3 * 2**20, transcendentals=2**17),
            name="conv_block",
        )(*(pltpu.with_memory_space_constraint(x, pltpu.HBM) for x in (features, conv_first, conv_second)))

    placed = P("tm", "lat", "lon", None)
    return jax.shard_map(local, mesh=mesh, in_specs=(placed, P(), P()), out_specs=placed, check_vma=False)
```

```python
import jax
import jax.numpy as jnp
from jax import lax
from jax.experimental import pallas as pl
from jax.experimental.pallas import tpu as pltpu
from jax.sharding import PartitionSpec as P

MESH = pl.DeviceIdType.MESH
BF16, F32, I32 = jnp.bfloat16, jnp.float32, jnp.int32
F0P, F1P, F0, F1, H0P, H1P, H0, H1 = range(8)
NEXT = {F0: F0P, F1: F1P, H0: H0P, H1: H1P}
E, W, U, UE, UW, D, DE, DW = range(8)
STEP = {E: (1, 0), W: (-1, 0), U: (0, -1), UE: (1, -1), UW: (-1, -1), D: (0, 1), DE: (1, 1), DW: (-1, 1)}
BACK = {E: W, W: E, U: D, D: U, UE: DW, DW: UE, UW: DE, DE: UW}
RIM = {E: 0, W: 1, DE: 2, DW: 3, UE: 4, UW: 5}
T = 16


def block(groups, tiles_lon, tiles_lat, f_ref, k1_ref, k2_ref, o_ref, xc, xl, xr, pack, rim, halo, w1, w2,
          acc_in, acc_out, acc, zsend, zrecv, lsend, lrecv, load, entered):
    tm, lon, lat = lax.axis_index("tm"), lax.axis_index("lon"), lax.axis_index("lat")
    rows, cols, chan = f_ref.shape[1:]
    has_prev, has_next, has_up, has_down = tm > 0, tm < groups - 1, lat > 0, lat < tiles_lat - 1

    ring = tiles_lon // 2

    def lateness(at):
        y = lax.rem(at, ring)
        return jnp.minimum(y, ring - y)

    east, west = lax.rem(lon + 1, tiles_lon), lax.rem(lon + tiles_lon - 1, tiles_lon)
    earlier_e, earlier_w = lateness(east) < lateness(lon), lateness(west) < lateness(lon)
    later_e, later_w = jnp.logical_not(earlier_e), jnp.logical_not(earlier_w)
    far_e, far_w = lax.rem(lon, ring) == ring - 1, lax.rem(lon, ring) == 0
    near_e, near_w = jnp.logical_not(far_e), jnp.logical_not(far_w)
    up, down = lax.rem(lat + tiles_lat - 1, tiles_lat), lax.rem(lat + 1, tiles_lat)

    def device(d):
        step_lon, step_lat = STEP[d]
        to = {}
        if step_lon:
            to["lon"] = east if step_lon > 0 else west
        if step_lat:
            to["lat"] = down if step_lat > 0 else up
        return to

    def toward(ds, *runs):
        def some(rise):
            return [d for d in ds if STEP[d][1] == rise]

        def all_of(ds):
            for run in runs:
                for d in ds:
                    run(d)

        all_of(some(0))
        for rise, cond in ((-1, has_up), (1, has_down)):
            if some(rise):
                pl.when(cond)(lambda rise=rise: all_of(some(rise)))

    barrier = pltpu.get_barrier_semaphore()

    def greet(d):
        pl.semaphore_signal(barrier, inc=1, device_id=device(d), device_id_type=MESH)

    @pl.when(has_prev)
    def _():
        pl.semaphore_signal(barrier, inc=1, device_id={"tm": tm - 1}, device_id_type=MESH)

    origin = jnp.logical_and(tm == 0, jnp.logical_and(lon == 0, lat == 0))
    awake = jnp.logical_not(origin)
    lon_of, lat_of = {0: lon, 1: east, -1: west}, {0: lat, 1: down, -1: up}

    def to_origin(d):
        x, y = STEP[d]
        return jnp.logical_and(tm == 0, jnp.logical_and(lon_of[x] == 0, lat_of[y] == 0))

    def either(a, b):
        return True if a is True or b is True else jnp.logical_or(a, b)

    def greets_me(d):
        first = {U: True, D: True, E: either(near_e, earlier_e), W: near_w}.get(d, earlier_e if STEP[d][0] > 0 else earlier_w)
        if d in (D, DE, DW):
            return either(origin, first)
        return jnp.logical_and(either(origin, first), jnp.logical_not(to_origin(d)))

    def i_greet(d):
        first = {U: True, D: True, E: near_e, W: True}.get(d, later_e if STEP[d][0] > 0 else later_w)
        if d in (D, DE, DW):
            return jnp.logical_and(awake, first)
        return jnp.logical_and(awake, either(first, to_origin(d)))

    def toward_if(cond, ds, *runs):
        toward(ds, *[lambda d, run=run: pl.when(cond(d))(lambda: run(d)) for run in runs])

    toward_if(i_greet, range(8), greet)

    opposite, across, relay = (lax.rem(lon + k, tiles_lon) for k in (ring, ring + 1, ring - 1))

    def relays(d):
        return jnp.logical_not(jnp.logical_and(tm == 0, jnp.logical_and(across == 0, lat_of[STEP[d][1]] == 0)))

    @pl.when(far_e)
    def _():
        pl.semaphore_signal(barrier, inc=1, device_id={"lon": opposite}, device_id_type=MESH)

    @pl.when(jnp.logical_and(far_w, awake))
    def _():
        toward((W, UW, DW), lambda d: pl.semaphore_signal(
            barrier, inc=1, device_id={**device(d), "lon": relay}, device_id_type=MESH))

    EAST, WEST = (E, UE, DE), (W, UW, DW)
    from_last, to_first = jnp.logical_and(lon == 0, has_prev), jnp.logical_and(lon == tiles_lon - 1, has_next)

    @pl.when(from_last)
    def _():
        toward(WEST, lambda d: pl.semaphore_signal(
            barrier, inc=1, device_id={"tm": tm - 1, **device(d)}, device_id_type=MESH))


    over = tiles_lat // 2
    from_over, to_over = jnp.logical_and(lat == over - 1, has_prev), jnp.logical_and(lat == over, has_next)

    @pl.when(from_over)
    def _():
        pl.semaphore_signal(barrier, inc=1, device_id={"tm": tm - 1, "lat": down}, device_id_type=MESH)

    loads = [
        pltpu.make_async_copy(f_ref.at[1], xc.at[F1, pl.ds(1, rows)], load.at[0]),
        pltpu.make_async_copy(f_ref.at[0], xc.at[F0, pl.ds(1, rows)], load.at[1]),
        pltpu.make_async_copy(k1_ref, w1, load.at[2]),
        pltpu.make_async_copy(k2_ref, w2, load.at[3]),
    ]
    for copy in loads:
        copy.start()

    def remote(src, dst, sems, i, to):
        return pltpu.make_async_remote_copy(
            src_ref=src, dst_ref=dst, send_sem=sems[0].at[i], recv_sem=sems[1].at[i], device_id=to, device_id_type=MESH)

    both, past = pl.ds(F0, 2), pl.ds(F0P, 2)
    left, inner, right = pl.ds(0, T), pl.ds(T, cols - 2 * T), pl.ds(cols - T, T)

    PACKS, F1_TOP, F1_LOW, F1_MID, F0_TOP, F0_LOW, F0_MID = range(7)
    H1_HALO, H1_IN, H1_TOP, H1_LOW, H1_LEFT, H1_RIGHT, H0_HALO, H0_TOP, H0_LOW, H0_MID = range(7, 17)

    def forward(i):
        def at(s, *where):
            return xc.at[(s, *where)], xc.at[(NEXT[s], *where)]

        mid = pl.ds(2, rows - 2)
        src, dst = {
            PACKS: lambda: (pack.at[both], pack.at[past]),
            F1_TOP: lambda: at(F1, 1), F1_LOW: lambda: at(F1, rows), F1_MID: lambda: at(F1, mid),
            F0_TOP: lambda: at(F0, 1), F0_LOW: lambda: at(F0, rows), F0_MID: lambda: at(F0, mid),
            H1_HALO: lambda: (halo.at[H1 - 4, 0], halo.at[H1P - 4, 0]),
            H1_IN: lambda: at(H1, mid, inner), H1_TOP: lambda: at(H1, 1), H1_LOW: lambda: at(H1, rows),
            H1_LEFT: lambda: at(H1, mid, left), H1_RIGHT: lambda: at(H1, mid, right),
            H0_HALO: lambda: (halo.at[H0 - 4, 0], halo.at[H0P - 4, 0]),
            H0_TOP: lambda: at(H0, 1), H0_LOW: lambda: at(H0, rows), H0_MID: lambda: at(H0, mid),
        }[i]()
        return remote(src, dst, (zsend, zrecv), i, {"tm": lax.rem(tm + 1, groups)})

    def send_on(*parts):
        pl.when(has_next)(lambda: [forward(p).start() for p in parts] and None)

    def arrived(*parts):
        pl.when(has_prev)(lambda: [forward(p).wait_recv() for p in parts] and None)

    def own(d):
        if d in RIM:
            src, dst = pack.at[both, int(STEP[d][0] > 0)], rim.at[both, RIM[d]]
        else:
            src, dst = xc.at[both, 1 if d == U else rows], xc.at[both, rows + 1 if d == U else 0]
        return remote(src, dst, (lsend, lrecv), d, device(d))

    def past_pack(d):
        return remote(pack.at[past, int(STEP[d][0] > 0)], rim.at[past, RIM[d]], (lsend, lrecv), 8 + d, device(d))

    def direct_pack(d):
        return remote(
            pack.at[both, 1], rim.at[past, RIM[d]], (lsend, lrecv), 8 + d, {"tm": lax.rem(tm + 1, groups), **device(d)})

    def row(s):
        base = {F1P: 8, F0P: 16}.get(s, 24 + 4 * (s - 4))

        def make(d):
            return remote(
                xc.at[s, 1 if d == U else rows], xc.at[s, rows + 1 if d == U else 0],
                (lsend, lrecv), base + (d if s < H0P else int(d == D)), device(d))
        return make

    def halo_of(s):
        def make(d):
            return remote(
                halo.at[s - 4, 0], halo.at[s - 4, 2 if d == U else 1],
                (lsend, lrecv), 26 + 4 * (s - 4) + int(d == D), device(d))
        return make

    def straight(s):
        to, base = {"tm": lax.rem(tm + 1, groups), "lat": up}, {F1: 10, F0: 18}.get(s, 24 + 4 * (NEXT[s] - 4))
        copies = [remote(xc.at[s, 1], xc.at[NEXT[s], rows + 1], (lsend, lrecv), base, to)]
        if s > H1P:
            copies.append(remote(halo.at[s - 4, 0], halo.at[NEXT[s] - 4, 2], (lsend, lrecv), base + 2, to))
        return copies

    def go_straight(s):
        pl.when(to_over)(lambda: [copy.start() for copy in straight(s)] and None)

    def gone_straight(*ss):
        pl.when(to_over)(lambda: [copy.wait_send() for s in ss for copy in straight(s)] and None)

    def pass_on(*runs):
        toward((D,), *runs)
        pl.when(lat != over)(lambda: toward((U,), *runs))

    def send(*makes):
        return [lambda d, make=make: make(d).start() for make in makes]

    def receive(*makes):
        return [lambda d, make=make: make(BACK[d]).wait_recv() for make in makes]

    def sent(*makes):
        return [lambda d, make=make: make(d).wait_send() for make in makes]

    def if_past(run):
        pl.when(has_prev)(run)

    ROWS, SIDES = (U, D), (E, UE, DE, W, UW, DW)

    @pl.when(jnp.logical_not(has_prev))
    def _():
        for s in (F0P, F1P, H0P, H1P):
            xc[s] = jnp.zeros(xc.shape[1:], BF16)
        pack[past] = jnp.zeros((2, *pack.shape[1:]), BF16)
        rim[past] = jnp.zeros((2, *rim.shape[1:]), BF16)
        halo[0:2] = jnp.zeros((2, *halo.shape[1:]), BF16)

    @pl.when(jnp.logical_not(has_up))
    def _():
        for s in range(8):
            xc[s, 0] = jnp.zeros((cols, chan), BF16)
        for s in range(4):
            rim[s, 2:4] = jnp.zeros((2, 2 * rows, chan), BF16)
            halo[s, 1] = jnp.zeros((2 * rows, chan), BF16)

    @pl.when(jnp.logical_not(has_down))
    def _():
        for s in range(8):
            xc[s, rows + 1] = jnp.zeros((cols, chan), BF16)
        for s in range(4):
            rim[s, 4:6] = jnp.zeros((2, 2 * rows, chan), BF16)
            halo[s, 2] = jnp.zeros((2 * rows, chan), BF16)

    def make_pack(s):
        for half, at in ((0, 0), (1, cols - T)):
            tile = [xc[s, r, at:at + T] for r in range(1, rows + 1)]
            js = (0, 1) if half == 0 else (T - 2, T - 1)
            pack[s, half] = jnp.concatenate([x[j:j + 1] for j in js for x in tile], axis=0)

    def beside(s, r):
        if s < H0P:
            if r == 0:
                return rim[s, 2, 2 * rows - 1:], rim[s, 3, rows - 1:rows]
            if r == rows + 1:
                return rim[s, 4, rows:rows + 1], rim[s, 5, 0:1]
            return rim[s, 0, rows + r - 1:rows + r], rim[s, 1, r - 1:r]
        if r == 0:
            return halo[s - 4, 1, rows - 1:rows], halo[s - 4, 1, 2 * rows - 1:]
        if r == rows + 1:
            return halo[s - 4, 2, 0:1], halo[s - 4, 2, rows:rows + 1]
        return halo[s - 4, 0, r - 1:r], halo[s - 4, 0, rows + r - 1:rows + r]

    def shift_in(s):
        for r in range(1, rows + 1):
            x = xc[s, r]
            xl[s, r, T:cols - T] = x[T - 1:cols - T - 1]
            xr[s, r, T:cols - T] = x[T + 1:cols - T + 1]

    def shift_out(s):
        for r in range(rows + 2):
            before, after = beside(s, r)
            x = xc[s, r]
            if r in (0, rows + 1):
                xl[s, r, T:cols - T] = x[T - 1:cols - T - 1]
                xr[s, r, T:cols - T] = x[T + 1:cols - T + 1]
            xl[s, r, 0:T] = jnp.concatenate([before, x[:T - 1]], axis=0)
            xl[s, r, cols - T:] = x[cols - T - 1:cols - 1]
            xr[s, r, 0:T] = x[1:T + 1]
            xr[s, r, cols - T:] = jnp.concatenate([x[cols - T + 1:], after], axis=0)

    def shift_all(s):
        for r in range(rows + 2):
            before, after = beside(s, r)
            x = xc[s, r]
            xl[s, r] = jnp.concatenate([before, x[:cols - 1]], axis=0)
            xr[s, r] = jnp.concatenate([x[1:], after], axis=0)

    def halo_taps(s):
        def column(above, mid, below):
            above, mid, below = above.astype(F32), mid.astype(F32), below.astype(F32)
            return (jnp.concatenate([above, mid[:rows - 1]], axis=0), mid, jnp.concatenate([mid[1:], below], axis=0))

        def rim_column(at, side):
            k = side
            return column(rim[s, k + 2, at + rows - 1:at + rows], rim[s, k, at:at + rows], rim[s, k + 4, at:at + 1])

        first = column(xc[s, 0, 0:1], pack[s, 0, 0:rows], xc[s, rows + 1, 0:1])
        last = column(xc[s, 0, cols - 1:], pack[s, 1, rows:], xc[s, rows + 1, cols - 1:])
        wests = (rim_column(0, 0), rim_column(rows, 0), first)
        easts = (last, rim_column(0, 1), rim_column(rows, 1))
        return jnp.concatenate(
            [jnp.concatenate([wests[c][b], easts[c][b]], axis=0).astype(BF16) for b in range(3) for c in range(3)], axis=1)

    MID, INNER = slice(1, rows - 1), slice(T, cols - T)
    IN = ((MID, INNER),)
    OUT = ((slice(0, rows), slice(0, T)), (slice(0, rows), slice(cols - T, cols)), (slice(0, 1), INNER), (slice(rows - 1, rows), INNER))
    ALL = ((slice(0, rows), slice(0, cols)),)

    def taken(ref, s, b, cuts):
        some = [ref[s, r.start + b:r.stop + b, c].reshape(-1, chan) for r, c in cuts]
        return some[0] if len(some) == 1 else jnp.concatenate(some, axis=0)

    def taps(s, w, times, cuts):
        x = jnp.concatenate([taken(ref, s, b, cuts) for b in range(3) for ref in (xl, xc, xr)], axis=1)
        if cuts is OUT:
            x = jnp.concatenate([x, halo_taps(s)], axis=0)
        k = jnp.concatenate([w[a].reshape(9 * chan, chan) for a in times], axis=1)
        return jnp.dot(x, k, preferred_element_type=F32)

    def shift(s, cuts):
        (shift_in if cuts is IN else shift_out if cuts is OUT else shift_all)(s)

    def own_later(s, w, acc, cuts):
        shift(s, cuts)
        acc[:, chan:] = taps(s, w, (2,), cuts)

    def own_earlier(s, w, acc, cuts):
        shift(s, cuts)
        v = taps(s, w, (2, 1), cuts)
        acc[:, :chan] = v[:, :chan]
        acc[:, chan:] += v[:, chan:]

    def past_later(s, w, acc, cuts):
        shift(s, cuts)
        v = acc[...] + taps(s, w, (1, 0), cuts)
        acc[:, :chan] = v[:, :chan]
        return v[:, chan:]

    def past_earlier(s, w, acc, cuts):
        shift(s, cuts)
        return acc[:, :chan] + taps(s, w, (0,), cuts)

    def silu(v):
        half = 0.5 * v
        return (half + half * jnp.tanh(half)).astype(BF16)

    def hidden_part(s, h, cuts):
        at = 0
        for r, c in cuts:
            high, wide = r.stop - r.start, c.stop - c.start
            xc[s, r.start + 1:r.stop + 1, c] = h[at:at + high * wide].reshape(high, wide, chan)
            at += high * wide
        return at

    def hidden_in(s, v):
        hidden_part(s, silu(v), IN)

    def hidden_out(s, v):
        h = silu(v)
        at = hidden_part(s, h, OUT)
        halo[s - 4, 0] = h[at:]

    def result(t, v):
        x = xc[(F0, F1)[t], 1:rows + 1].reshape(-1, chan).astype(F32) + v
        o_ref[t] = x.astype(BF16).reshape(rows, cols, chan)

    for s, copy in ((F1, loads[0]), (F0, loads[1])):
        copy.wait()
        make_pack(s)

    def count(d):
        there = (has_up, True, has_down)[STEP[d][1] + 1]
        return (greets_me(d) if there is True else jnp.logical_and(there, greets_me(d))).astype(I32)

    pl.semaphore_wait(
        barrier, has_next.astype(I32) + sum(count(d) for d in range(8))
        + far_e.astype(I32) * (1 + relays(E).astype(I32) + jnp.logical_and(has_up, relays(UE)).astype(I32)
                               + jnp.logical_and(has_down, relays(DE)).astype(I32))
        + to_over.astype(I32) + to_first.astype(I32) * (1 + has_up.astype(I32) + has_down.astype(I32)))

    send_on(PACKS)
    pl.when(to_first)(lambda: toward(EAST, *send(direct_pack)))
    send_on(F1_TOP, F1_LOW)
    go_straight(F1)
    send_on(F1_MID, F0_TOP, F0_LOW)
    go_straight(F0)
    send_on(F0_MID)

    def tell(d):
        to = device(d)
        if d in EAST:
            to["lon"] = jnp.where(far_e, across, east)
        pl.semaphore_signal(entered.at[BACK[d]], inc=1, device_id=to, device_id_type=MESH)

    def i_tell(d):
        quiet = jnp.logical_not(i_greet(d))
        if d in EAST:
            return jnp.where(far_e, relays(d), quiet)
        return jnp.logical_and(quiet, awake) if d in WEST else quiet

    helper = jnp.logical_and(tm == 0, jnp.logical_and(lon == 0, lat == 1))

    def direct(d):
        if d not in (E, UE):
            return True
        return jnp.logical_not(jnp.logical_and(to_origin(d), lon == tiles_lon - 1))

    def helped():
        return [
            pltpu.make_async_remote_copy(
                src_ref=rim.at[both, src], dst_ref=rim.at[both, dst], send_sem=lsend.at[40 + i], recv_sem=lrecv.at[d],
                device_id={"lat": up}, device_id_type=MESH)
            for i, (src, dst, d) in enumerate(((RIM[DE], RIM[E], E), (RIM[E], RIM[UE], UE)))]

    def told(d):
        pl.semaphore_wait(entered.at[d], 1)

    toward_if(i_tell, range(8), tell)

    def known(ds, *runs):
        toward(ds, lambda d: pl.when(greets_me(d))(lambda: [run(d) for run in runs] and None))

    def late(d):
        return False if d in (D, DE, DW) else to_origin(d)

    def soon(d):
        return jnp.logical_not(jnp.logical_or(greets_me(d), late(d)))

    def last(d):
        slow = jnp.logical_and(jnp.logical_not(greets_me(d)), late(d))
        return slow if direct(d) is True else jnp.logical_and(slow, direct(d))

    def send_past_pack(d):
        if d in EAST:
            pl.when(jnp.logical_and(has_prev, inland))(lambda: past_pack(d).start())
        else:
            if_past(lambda: past_pack(d).start())

    def after_word(cond):
        def run(d):
            told(d)
            own(d).start()
            if d in RIM:
                send_past_pack(d)
        toward(ROWS + SIDES, lambda d: pl.when(cond(d))(lambda: run(d)))

    known(ROWS + SIDES, *send(own))
    loads[2].wait()
    own_later(F1, w1, acc_in, IN)
    own_earlier(F0, w1, acc_in, IN)
    arrived(PACKS)
    if_past(lambda: known(WEST, *send(past_pack)))
    inland = lon < tiles_lon - 1
    pl.when(jnp.logical_and(has_prev, inland))(lambda: known(EAST, *send(past_pack)))
    arrived(F1_TOP, F1_LOW)
    if_past(lambda: pass_on(*send(row(F1P))))
    after_word(soon)
    arrived(F1_MID)
    hidden_in(H1, past_later(F1P, w1, acc_in, IN))
    send_on(H1_IN)
    arrived(F0_TOP, F0_LOW)
    if_past(lambda: pass_on(*send(row(F0P))))
    after_word(last)

    toward(ROWS + SIDES, *receive(own))
    pl.when(helper)(lambda: [copy.start() for copy in helped()] and None)
    own_later(F1, w1, acc_out, OUT)
    own_earlier(F0, w1, acc_out, OUT)

    def inner_earlier():
        arrived(F0_MID)
        hidden_in(H0, past_earlier(F0P, w1, acc_in, IN))

    far = jnp.logical_or(far_e, far_w)
    pl.when(far)(inner_earlier)
    if_past(lambda: toward(SIDES, *receive(past_pack)))
    if_past(lambda: toward(ROWS, *receive(row(F1P))))
    hidden_out(H1, past_later(F1P, w1, acc_out, OUT))
    send_on(H1_HALO, H1_TOP, H1_LOW)
    go_straight(H1)
    send_on(H1_LEFT, H1_RIGHT)
    toward(ROWS, *send(row(H1), halo_of(H1)))
    pl.when(jnp.logical_not(far))(inner_earlier)
    if_past(lambda: toward(ROWS, *receive(row(F0P))))
    hidden_out(H0, past_earlier(F0P, w1, acc_out, OUT))
    send_on(H0_HALO, H0_TOP, H0_LOW)
    go_straight(H0)
    send_on(H0_MID)
    toward(ROWS, *send(row(H0), halo_of(H0)))

    loads[3].wait()
    pl.when(has_next)(lambda: [forward(p).wait_send() for p in range(H1_HALO)] and None)
    toward((U, D, DE, W, UW, DW), *sent(own))
    toward_if(direct, (E, UE), *sent(own))
    pl.when(helper)(lambda: [copy.wait_send() for copy in helped()] and None)
    pl.when(to_first)(lambda: toward(EAST, *sent(direct_pack)))
    gone_straight(F1, F0)

    @pl.when(has_prev)
    def _():
        toward(WEST, *sent(past_pack))
        pl.when(inland)(lambda: toward(EAST, *sent(past_pack)))
        pass_on(*sent(row(F1P), row(F0P)))

    arrived(H1_HALO, H1_TOP, H1_LOW)
    if_past(lambda: pass_on(*send(row(H1P), halo_of(H1P))))
    toward(ROWS, *receive(row(H1), halo_of(H1)))
    own_later(H1, w2, acc, ALL)
    arrived(H0_HALO, H0_TOP, H0_LOW)
    if_past(lambda: pass_on(*send(row(H0P), halo_of(H0P))))
    toward(ROWS, *receive(row(H0), halo_of(H0)))
    own_earlier(H0, w2, acc, ALL)
    pl.when(has_next)(lambda: [forward(p).wait_send() for p in range(H1_HALO, 17)] and None)
    gone_straight(H1, H0)
    toward(ROWS, *sent(row(H0), halo_of(H0), row(H1), halo_of(H1)))
    if_past(lambda: toward(ROWS, *receive(row(H1P), halo_of(H1P))))
    arrived(H1_IN, H1_LEFT, H1_RIGHT)
    result(1, past_later(H1P, w2, acc, ALL))
    arrived(H0_MID)
    if_past(lambda: toward(ROWS, *receive(row(H0P), halo_of(H0P))))
    result(0, past_earlier(H0P, w2, acc, ALL))
    if_past(lambda: pass_on(*sent(row(H1P), halo_of(H1P), row(H0P), halo_of(H0P))))


def solution(mesh):
    groups, tiles_lon, tiles_lat = mesh.shape["tm"], mesh.shape["lon"], mesh.shape["lat"]

    def local(features, conv_first, conv_second):
        frames, rows, cols, chan = features.shape
        frame = (8, rows + 2, cols, chan)
        inner = (cols - 2 * T) * (rows - 2)
        outer = rows * cols - inner + 2 * rows

        def kernel(*refs):
            block(groups, tiles_lon, tiles_lat, *refs)

        return pl.pallas_call(
            kernel,
            out_shape=pltpu.VMEM(features.shape, BF16),
            in_specs=[pl.BlockSpec(memory_space=pltpu.HBM)] * 3,
            out_specs=pl.BlockSpec(memory_space=pltpu.VMEM),
            scratch_shapes=[
                pltpu.VMEM(frame, BF16),
                pltpu.VMEM(frame, BF16),
                pltpu.VMEM(frame, BF16),
                pltpu.VMEM((4, 2, 2 * rows, chan), BF16),
                pltpu.VMEM((4, 6, 2 * rows, chan), BF16),
                pltpu.VMEM((4, 3, 2 * rows, chan), BF16),
                pltpu.VMEM(conv_first.shape, BF16),
                pltpu.VMEM(conv_second.shape, BF16),
                pltpu.VMEM((inner, 2 * chan), F32),
                pltpu.VMEM((outer, 2 * chan), F32),
                pltpu.VMEM((rows * cols, 2 * chan), F32),
                pltpu.SemaphoreType.DMA((17,)),
                pltpu.SemaphoreType.DMA((17,)),
                pltpu.SemaphoreType.DMA((42,)),
                pltpu.SemaphoreType.DMA((40,)),
                pltpu.SemaphoreType.DMA((4,)),
                pltpu.SemaphoreType.REGULAR((8,)),
            ],
            compiler_params=pltpu.CompilerParams(
                collective_id=0, has_side_effects=True, vmem_limit_bytes=32 * 2**20),
            cost_estimate=pl.CostEstimate(
                flops=4 * frames * rows * cols * 27 * chan * chan, bytes_accessed=3 * 2**20, transcendentals=2**17),
            name="conv_block",
        )(*(pltpu.with_memory_space_constraint(x, pltpu.HBM) for x in (features, conv_first, conv_second)))

    placed = P("tm", "lat", "lon", None)
    return jax.shard_map(local, mesh=mesh, in_specs=(placed, P(), P()), out_specs=placed, check_vma=False)
```
